32 devices in a mesh: drift: 4 (over x, core), beam: 8 (over z, y).
Axes of the slice: x: 2, y: 2, z: 4, core: 2. Of those that a mesh axis runs over, the one named last changes fastest.
Arguments:
- features: bfloat16 [32, 32, 128, 128], P('drift', None, 'beam'), may hold values from -6 to 6
- occupied: int32 [4, 16, 16], P('drift', 'beam'), may hold values 0 or 1
- voxel_fragment: int32 [32, 128, 128], P('drift', 'beam'), may hold values from 0 to 2047, as said below
- conv_weight: bfloat16 [32, 864], replicated, may hold values from -0.21875 to 0.21875
- embed_weight: bfloat16 [32, 256], replicated, may hold values from -6 to 6
- message_weight: bfloat16 [256, 256], replicated, may hold values from -0.375 to 0.375
- update_weight: bfloat16 [256, 256], replicated, may hold values from -0.375 to 0.375
- edge_source: int32 [32768], P(('drift', 'beam')), may hold values from 0 to 2047
- edge_target: int32 [32768], P(('drift', 'beam')), may hold values from 0 to 255
- out_cotangent: bfloat16 [8192, 256], P(('drift', 'beam')), may hold values from -6 to 6
Outputs:
- fragment_out: bfloat16 [8192, 256], P(('drift', 'beam'))
- grad_features: float32 [32, 32, 128, 128], P('drift', None, 'beam')
- grad_conv: float32 [32, 864], replicated
The draws below stay inside these ranges and needn't reach their ends.
Inputs may be any that keep to these rules, and one draw needn't show every extreme that they name: `voxel_fragment`: index among the 2048 fragments of the voxel's drift row.
All inputs are finite; a program needn't handle non-finite values. No bound on the sum of `occupied` on one device may be relied on, other than what follows from the above.
Results may differ from the reference program's by a relative error of at most 0.01.
Values may be sent and summed in bfloat16 or wider, within the bound.
No kernel may reach another device: no remote copies, remote signals or barrier semaphores. Data moves between devices by JAX's collectives and lax.ppermute only.
A program may use at most 64 MiB of HBM per device.

```python
import jax
import jax.numpy as jnp
from jax import lax

C = 32
HID = 256
BLOCK = 8
TX = 8
TY = 16
FRAG_DEV = 256
EDGE_DEV = 1024
NX = 32
NY = 128
NZ = 128
FRAG_ROW = 2048
FRAGS = 8192
EDGES = 32768
N_BEAM = 8


def draw_voxel_fragment(key, part):
    tiles = NY // TY
    shape = (NX, NY, NZ)
    column = (jnp.arange(NY, dtype=jnp.int32) // TY)[None, :, None]
    near = jax.random.randint(jax.random.fold_in(key, 11), shape, -1, 2)
    far = jax.random.randint(jax.random.fold_in(key, 12), shape, 0, tiles)
    pick = jax.random.randint(jax.random.fold_in(key, 13), shape, 0, 10)
    owner = jnp.where(pick < 7, (column + near + tiles) % tiles, far)
    first = jax.random.randint(jax.random.fold_in(key, 14), shape, 0, FRAG_DEV)
    second = jax.random.randint(jax.random.fold_in(key, 15), shape, 0, FRAG_DEV)
    local = first * second // FRAG_DEV
    return (owner * FRAG_DEV + local).astype(jnp.int32)


def with_ends(values, rng, least, largest):
    longest = values.shape.index(max(values.shape))
    spots = []
    for shift in (0, 1):
        where = [jax.random.randint(jax.random.fold_in(rng, axis), (), 0, length) for axis, length in enumerate(values.shape)]
        where[longest] = (where[longest] + shift) % values.shape[longest]
        spots.append(tuple(where))
    return values.at[spots[0]].set(least).at[spots[1]].set(largest)


def steps_of(key, extent, shards, least, high):
    gain = 1.0
    for position, blocks in shards:
        draws = jax.random.uniform(jax.random.fold_in(jax.random.fold_in(key, 6), position), (blocks,), jnp.float32, least / len(shards), high / len(shards))
        gain = gain * jnp.repeat(jnp.exp(draws), extent[position] // blocks).reshape((-1,) + (1,) * (len(extent) - 1 - position))
    return gain


def normal_values(key, dims, deviation, limit, shards=(), held_as=jnp.bfloat16):
    drawn = jax.random.normal(key, dims, jnp.float32) * deviation
    if len(shards) > 0:
        drawn = steps_of(key, dims, shards, -0.22, 0.18) * drawn
    return jnp.clip(drawn, min=-limit, max=limit).astype(held_as)


def setup_inputs(seed: int = 0) -> dict:
    streams_of = jax.random.split(jax.random.key(seed), 11)
    return {
        "features": normal_values(streams_of[0], (NX, C, NY, NZ), 1.0, 6.0, ((0, 4), (2, 8))),
        "occupied": with_ends((jax.random.randint(streams_of[1], (NX // BLOCK, NY // BLOCK, NZ // BLOCK), 0, 8) < 5).astype(jnp.int32), jax.random.fold_in(streams_of[1], 1), 0, 1),
        "voxel_fragment": draw_voxel_fragment(jax.random.fold_in(streams_of[10], 71), 0),
        "conv_weight": normal_values(streams_of[3], (C, 27 * C), (27 * C) ** -0.5, 0.21875),
        "embed_weight": normal_values(streams_of[4], (C, HID), 1 ** -0.5, 6.0),
        "message_weight": normal_values(streams_of[5], (HID, HID), HID ** -0.5, 0.375),
        "update_weight": normal_values(streams_of[6], (HID, HID), HID ** -0.5, 0.375),
        "edge_source": with_ends(jax.random.randint(streams_of[7], (EDGES,), 0, FRAG_ROW), jax.random.fold_in(streams_of[7], 1), 0, FRAG_ROW - 1).astype(jnp.int32),
        "edge_target": with_ends(jax.random.randint(streams_of[8], (EDGES,), 0, FRAG_DEV), jax.random.fold_in(streams_of[8], 1), 0, FRAG_DEV - 1).astype(jnp.int32),
        "out_cotangent": normal_values(streams_of[9], (FRAGS, HID), 1.0, 6.0, ((0, 32),)),
    }


def slope(value):
    sig = jax.nn.sigmoid(value)
    return sig * (1.0 + value * (1.0 - sig))


def columns(padded, row):
    channels = padded.shape[1]
    height = padded.shape[2] - 2
    depth = padded.shape[3] - 2
    anchor = jnp.zeros((), jnp.int32)
    start_row = anchor + row
    pieces = []
    for off_a in range(3):
        for off_b in range(3):
            for off_c in range(3):
                index = (start_row + off_a, anchor, anchor + off_b, anchor + off_c)
                piece = lax.dynamic_slice(padded, index, (1, channels, height, depth))
                pieces.append(piece.reshape(channels, height * depth))
    return jnp.concatenate(pieces, 0)


def convolve(padded, weight):
    rows = padded.shape[0] - 2
    height = padded.shape[2] - 2
    depth = padded.shape[3] - 2
    wide = weight.astype(jnp.float32)

    def one_row(row):
        cols = columns(padded, row).astype(jnp.float32)
        return jnp.dot(wide, cols, precision=lax.Precision.HIGHEST)

    result = lax.map(one_row, jnp.arange(rows, dtype=jnp.int32))
    return result.reshape(rows, weight.shape[0], height, depth)


def reference(features, occupied, voxel_fragment, conv_weight, embed_weight, message_weight, update_weight, edge_source, edge_target, out_cotangent):
    f32 = jnp.float32
    mask = jnp.repeat(jnp.repeat(jnp.repeat(occupied, BLOCK, 0), BLOCK, 1), BLOCK, 2).astype(f32)
    mask_four = mask[:, None]
    active = features * mask_four.astype(features.dtype)
    padded = jnp.pad(active, ((1, 1), (0, 0), (1, 1), (1, 1)))
    conv_out = convolve(padded, conv_weight)
    hidden = mask_four * (active.astype(f32) + jax.nn.silu(conv_out))
    row_of = jnp.arange(NX, dtype=jnp.int32) // TX
    frag_ids = (row_of[:, None, None] * FRAG_ROW + voxel_fragment).reshape(-1).astype(jnp.int32)
    by_voxel = hidden.transpose(0, 2, 3, 1).reshape(-1, C)
    sums = jax.ops.segment_sum(by_voxel, frag_ids, num_segments=FRAGS)
    counts = jax.ops.segment_sum(mask.reshape(-1), frag_ids, num_segments=FRAGS)
    divisor = jnp.maximum(counts, 1.0)[:, None]
    pooled = (sums / divisor).astype(jnp.bfloat16)
    pre_own = jnp.dot(pooled, embed_weight, preferred_element_type=f32)
    own = jax.nn.silu(pre_own).astype(jnp.bfloat16)
    device = jnp.arange(EDGES, dtype=jnp.int32) // EDGE_DEV
    drift_row = device // N_BEAM
    beam_col = device % N_BEAM
    src = (drift_row * FRAG_ROW + edge_source).astype(jnp.int32)
    dst = (drift_row * FRAG_ROW + beam_col * FRAG_DEV + edge_target).astype(jnp.int32)
    pre_msg = jnp.dot(own[src], message_weight, preferred_element_type=f32)
    messages = jax.nn.silu(pre_msg).astype(jnp.bfloat16)
    gathered = jax.ops.segment_sum(messages.astype(f32), dst, num_segments=FRAGS).astype(jnp.bfloat16)
    fragment_out = (own.astype(f32) + jnp.dot(gathered, update_weight, preferred_element_type=f32)).astype(jnp.bfloat16)
    back_agg = jnp.dot(out_cotangent, update_weight.T, preferred_element_type=f32).astype(jnp.bfloat16)
    back_pre = (back_agg[dst].astype(f32) * slope(pre_msg)).astype(jnp.bfloat16)
    back_src = jnp.dot(back_pre, message_weight.T, preferred_element_type=f32)
    back_own = out_cotangent.astype(f32) + jax.ops.segment_sum(back_src, src, num_segments=FRAGS)
    back_pooled = jnp.dot(back_own * slope(pre_own), embed_weight.astype(f32).T, precision=lax.Precision.HIGHEST)
    back_mean = back_pooled / divisor
    back_hidden = back_mean[frag_ids].reshape(NX, NY, NZ, C).transpose(0, 3, 1, 2)
    back_conv = (mask_four * back_hidden * slope(conv_out)).astype(jnp.bfloat16)
    padded_grad = jnp.pad(back_conv, ((1, 1), (0, 0), (1, 1), (1, 1)))
    flipped = conv_weight.reshape(C, 27, C)[:, ::-1, :].transpose(2, 1, 0).reshape(C, 27 * C)
    back_active = mask_four * back_hidden + convolve(padded_grad, flipped)
    grad_features = mask_four * back_active

    def accumulate(total, row):
        cols = columns(padded, row).astype(f32)
        slab = lax.dynamic_index_in_dim(back_conv, row, 0, keepdims=False).reshape(C, -1).astype(f32)
        term = lax.dot_general(slab, cols, (((1,), (1,)), ((), ())), precision=lax.Precision.HIGHEST)
        return total + term, None

    grad_conv, _ = lax.scan(accumulate, jnp.zeros((C, 27 * C), f32), jnp.arange(NX, dtype=jnp.int32))
    return fragment_out, grad_features, grad_conv
```

```python
import jax
import jax.numpy as jnp
from jax import lax
from jax.experimental import pallas as pl
from jax.experimental.pallas import tpu as pltpu
from jax.sharding import PartitionSpec as P

BLOCK = 8
REACH = 3
SPARE = 8
LIMIT = 56 * 1024 * 1024
bf16 = jnp.bfloat16
f32 = jnp.float32


def contract(left, right, dims):
    return lax.dot_general(left, right, ((dims[0], dims[1]), ((), ())), preferred_element_type=f32)


def plain(left, right):
    return contract(left, right, ((1,), (0,)))


def by_last(left, right):
    return contract(left, right, ((1,), (1,)))


def by_first(left, right):
    return contract(left, right, ((0,), (0,)))


def slope_of(value, sig):
    return sig * (1.0 + value * (1.0 - sig))


def one_hot(index, count):
    places = lax.broadcasted_iota(jnp.int32, (count, index.shape[-1]), 0)
    return jnp.where(places == index, 1.0, 0.0).astype(bf16)


def spread(values, owner, owners):
    parts = [jnp.where(owner == h, values, 0.0).astype(bf16) for h in range(owners)]
    return jnp.concatenate(parts, 0)


def pick(stacked, owner, owners):
    width = stacked.shape[0] // owners
    total = jnp.where(owner == 0, stacked[:width], 0.0)
    for h in range(1, owners):
        total = total + jnp.where(owner == h, stacked[h * width : (h + 1) * width], 0.0)
    return total


def store_taps(taps, row, first, tiles):
    count, channels, depth = tiles.shape
    flat = tiles.reshape(count * channels, depth)
    lane = lax.broadcasted_iota(jnp.int32, flat.shape, 1)
    before = jnp.where(lane == 0, 0.0, pltpu.roll(flat, 1, 1))
    after = jnp.where(lane == depth - 1, 0.0, pltpu.roll(flat, depth - 1, 1))
    for place, value in enumerate((before, flat, after)):
        taps[row, first : first + count, place * channels : (place + 1) * channels, :] = (
            value.reshape(count, channels, depth).astype(bf16)
        )


def columns(taps, row, first, count):
    wide = []
    for y in range(first, first + count):
        pieces = [taps[row + a, y + b] for a in range(REACH) for b in range(REACH)]
        wide.append(jnp.concatenate(pieces, 0))
    return jnp.concatenate(wide, 1)


def convolve_row(taps, weight, row, height):
    return jnp.concatenate(
        [plain(weight, columns(taps, row, y, 2)) for y in range(0, height, 2)], 1
    )


def forward_kernel(
    feat, x_low, x_high, y_low, y_high, mask, owner, local, weight, taps, slopes, partial, total
):
    rows, channels, height, depth = feat.shape
    owners, _, frag_dev = partial.shape

    def turned(block):
        return jnp.swapaxes(block.astype(f32), 0, 1)

    store_taps(taps, 0, 1, turned(x_low[...]))
    store_taps(taps, rows + 1, 1, turned(x_high[...]))

    def fill(x, _):
        tiles = turned(feat[x])
        live = mask[x]
        gates = [live[:, y * depth : (y + 1) * depth] for y in range(height)]
        gates = jnp.concatenate([jnp.broadcast_to(g, (1, channels, depth)) for g in gates], 0)
        store_taps(taps, x + 1, 1, tiles * gates)
        return 0

    lax.fori_loop(0, rows, fill, 0)

    def edges(x, _):
        store_taps(taps, x, 0, y_low[x].astype(f32)[None])
        store_taps(taps, x, height + 1, y_high[x].astype(f32)[None])
        return 0

    lax.fori_loop(0, rows + 2, edges, 0)
    total[...] = jnp.zeros_like(total)

    def one_row(x, _):
        conv = convolve_row(taps, weight[...], x, height)
        active = jnp.concatenate(
            [taps[x + 1, y + 1, channels : 2 * channels, :] for y in range(height)], 1
        )
        live = mask[x]
        sig = jax.nn.sigmoid(conv)
        hidden = live * (active.astype(f32) + conv * sig)
        slopes[x] = live * slope_of(conv, sig)
        tallies = lax.broadcasted_iota(jnp.int32, (total.shape[0] - owners * channels, 1), 0)
        heads = jnp.where(tallies == owner[x], live, 0.0).astype(bf16)
        rising = jnp.concatenate([spread(hidden, owner[x], owners), heads], 0)
        total[...] += by_last(rising, one_hot(local[x], frag_dev))
        return 0

    lax.fori_loop(0, rows, one_row, 0)
    for h in range(owners):
        partial[h, :channels] = total[h * channels : (h + 1) * channels]
        place = owners * channels + h
        tally = total[place : place + 1]
        partial[h, channels:] = jnp.broadcast_to(tally, (SPARE, frag_dev))


def pool_kernel(parts, pooled, divisor):
    sums = parts[0]
    for h in range(1, parts.shape[0]):
        sums = sums + parts[h]
    channels = pooled.shape[1]
    below = jnp.maximum(sums[channels:], 1.0)
    divisor[...] = below
    result = (sums[:channels] / below[:1]).astype(bf16)
    for h in range(pooled.shape[0]):
        pooled[h] = result


def fragment_kernel(
    table, mine, embed, message, update, cotangent, owner, local, target, out, partial, direct
):
    owners, channels, frag_dev = table.shape
    flat = table[...].reshape(owners * channels, frag_dev)
    from_local = one_hot(local[...], frag_dev)
    source = pick(plain(flat, from_local), owner[...], owners).astype(bf16)
    pre_source = by_first(source, embed[...])
    sig_source = jax.nn.sigmoid(pre_source)
    own_source = (pre_source * sig_source).astype(bf16)
    pre_msg = plain(own_source, message[...])
    sig_msg = jax.nn.sigmoid(pre_msg)
    messages = (pre_msg * sig_msg).astype(bf16)
    to_target = one_hot(target[...], frag_dev)
    gathered = plain(to_target, messages).astype(bf16)
    pre_own = by_first(mine[...], embed[...])
    sig_own = jax.nn.sigmoid(pre_own)
    own = (pre_own * sig_own).astype(bf16)
    out[...] = (own.astype(f32) + plain(gathered, update[...])).astype(bf16)
    back_agg = by_last(cotangent[...], update[...]).astype(bf16)
    back_edge = by_first(to_target, back_agg)
    back_pre = (back_edge * slope_of(pre_msg, sig_msg)).astype(bf16)
    back_source = by_last(back_pre, message[...]) * slope_of(pre_source, sig_source)
    back_pooled = by_last(embed[...], back_source.astype(bf16))
    scattered = by_last(spread(back_pooled, owner[...], owners), from_local)
    partial[...] = scattered.reshape(partial.shape).astype(partial.dtype)
    near = cotangent[...].astype(f32) * slope_of(pre_own, sig_own)
    rough = near.astype(bf16)
    rest = (near - rough.astype(f32)).astype(bf16)
    direct[...] = by_last(embed[...], rough) + by_last(embed[...], rest)


def mean_kernel(parts, direct, divisor, mean):
    total = direct[...]
    for h in range(parts.shape[0]):
        total = total + parts[h].astype(f32)
    result = (total / divisor[:1]).astype(bf16)
    for h in range(mean.shape[0]):
        mean[h] = result


def hidden_kernel(table, owner, local, mask, slopes, back_hidden, back_conv):
    owners, channels, frag_dev = table.shape
    rows, height, _, depth = back_conv.shape
    flat = table[...].reshape(owners * channels, frag_dev)

    def one_row(x, _):
        found = plain(flat, one_hot(local[x], frag_dev))
        hidden = pick(found, owner[x], owners)
        back_hidden[x] = mask[x] * hidden
        grad = (hidden * slopes[x]).astype(bf16)
        for y in range(height):
            back_conv[x, y] = grad[:, y * depth : (y + 1) * depth]
        return 0

    lax.fori_loop(0, rows, one_row, 0)


def weight_kernel(taps, back_conv, grad):
    rows, height, _, _ = back_conv.shape
    grad[...] = jnp.zeros_like(grad)

    def one_row(x, _):
        total = None
        for y in range(0, height, 2):
            slab = jnp.concatenate([back_conv[x, y], back_conv[x, y + 1]], 1)
            term = by_last(slab, columns(taps, x, y, 2))
            total = term if total is None else total + term
        grad[...] += total
        return 0

    lax.fori_loop(0, rows, one_row, 0)


def backward_kernel(
    back_conv, x_low, x_high, y_low, y_high, back_hidden, mask, weight, grad, taps
):
    rows, height, channels, depth = back_conv.shape
    store_taps(taps, 0, 1, x_low[...].astype(f32))
    store_taps(taps, rows + 1, 1, x_high[...].astype(f32))

    def fill(x, _):
        store_taps(taps, x + 1, 1, back_conv[x].astype(f32))
        return 0

    lax.fori_loop(0, rows, fill, 0)

    def edges(x, _):
        store_taps(taps, x, 0, y_low[x].astype(f32)[None])
        store_taps(taps, x, height + 1, y_high[x].astype(f32)[None])
        return 0

    lax.fori_loop(0, rows + 2, edges, 0)

    def one_row(x, _):
        result = mask[x] * (back_hidden[x] + convolve_row(taps, weight[...], x, height))
        tiles = [result[:, y * depth : (y + 1) * depth][None] for y in range(height)]
        grad[x] = jnp.swapaxes(jnp.concatenate(tiles, 0), 0, 1)
        return 0

    lax.fori_loop(0, rows, one_row, 0)


def call(kernel, shapes, *operands, scratch=()):
    return pl.pallas_call(
        kernel,
        out_shape=[jax.ShapeDtypeStruct(shape, kind) for shape, kind in shapes],
        scratch_shapes=list(scratch),
        compiler_params=pltpu.CompilerParams(vmem_limit_bytes=LIMIT),
    )(*operands)


def pass_on(low, high, axis):
    count = lax.axis_size(axis)
    up = [(i, i + 1) for i in range(count - 1)]
    down = [(i + 1, i) for i in range(count - 1)]
    return lax.ppermute(high, axis, up), lax.ppermute(low, axis, down)


def exchange(parts, axes):
    return lax.all_to_all(parts, axes, 0, 0, tiled=True)


def sum_everywhere(values, axes):
    count = lax.axis_size(axes)
    flat = values.reshape(-1)
    share = -(-flat.shape[0] // count)
    flat = jnp.pad(flat, (0, share * count - flat.shape[0])).reshape(count, share)
    mine = exchange(flat, axes).sum(0)
    back = exchange(jnp.broadcast_to(mine[None], flat.shape), axes)
    return back.reshape(-1)[: values.size].reshape(values.shape)


def body(
    features,
    occupied,
    voxel_fragment,
    conv_weight,
    embed_weight,
    message_weight,
    update_weight,
    edge_source,
    edge_target,
    out_cotangent,
):
    rows, channels, height, depth = features.shape
    frag_dev, hid = out_cotangent.shape
    owners = lax.axis_size("beam")
    edge_count = edge_source.shape[0]
    plane = height * depth
    mask = jnp.repeat(jnp.repeat(jnp.repeat(occupied, BLOCK, 0), BLOCK, 1), BLOCK, 2)
    gate = mask.astype(bf16)

    x_low, x_high = pass_on(
        features[0] * gate[0][None], features[-1] * gate[-1][None], "drift"
    )
    ends = []
    for y in (0, height - 1):
        side = features[:, :, y] * gate[:, None, y]
        ends.append(jnp.concatenate([x_low[None, :, y], side, x_high[None, :, y]], 0))
    y_low, y_high = pass_on(ends[0], ends[1], "beam")

    live = mask.astype(f32).reshape(rows, 1, plane)
    owner = (voxel_fragment // frag_dev).reshape(rows, 1, plane)
    local = (voxel_fragment % frag_dev).reshape(rows, 1, plane)
    heads = -(-owners // 16) * 16
    padded = (rows + 2, height + 2, REACH * channels, depth)
    taps, slopes, partial = call(
        forward_kernel,
        [
            (padded, bf16),
            ((rows, channels, plane), f32),
            ((owners, channels + SPARE, frag_dev), f32),
        ],
        features, x_low, x_high, y_low, y_high, live, owner, local, conv_weight,
        scratch=[pltpu.VMEM((owners * channels + heads, frag_dev), f32)],
    )
    spread_shape = (owners, channels, frag_dev)
    pooled, divisor = call(
        pool_kernel,
        [(spread_shape, bf16), ((SPARE, frag_dev), f32)],
        exchange(partial, "beam"),
    )
    table = exchange(pooled, "beam")
    fragment_out, back_parts, direct = call(
        fragment_kernel,
        [((frag_dev, hid), bf16), (spread_shape, f32), ((channels, frag_dev), f32)],
        table, pooled[0], embed_weight, message_weight, update_weight, out_cotangent,
        (edge_source // frag_dev).reshape(1, edge_count),
        (edge_source % frag_dev).reshape(1, edge_count),
        edge_target.reshape(1, edge_count),
    )
    (mean,) = call(
        mean_kernel, [(spread_shape, bf16)], exchange(back_parts, "beam"), direct, divisor
    )
    back_hidden, back_conv = call(
        hidden_kernel,
        [((rows, channels, plane), f32), ((rows, height, channels, depth), bf16)],
        exchange(mean, "beam"), owner, local, live, slopes,
    )
    gx_low, gx_high = pass_on(back_conv[0], back_conv[-1], "drift")
    ends = [
        jnp.concatenate([gx_low[None, y], back_conv[:, y], gx_high[None, y]], 0)
        for y in (0, height - 1)
    ]
    gy_low, gy_high = pass_on(ends[0], ends[1], "beam")
    (local_grad,) = call(weight_kernel, [(conv_weight.shape, f32)], taps, back_conv)
    taps_count = REACH * REACH * REACH
    flipped = (
        conv_weight.reshape(channels, taps_count, channels)[:, ::-1, :]
        .transpose(2, 1, 0)
        .reshape(channels, taps_count * channels)
    )
    (grad_features,) = call(
        backward_kernel,
        [(features.shape, f32)],
        back_conv, gx_low, gx_high, gy_low, gy_high, back_hidden, live, flipped,
        scratch=[pltpu.VMEM(padded, bf16)],
    )
    grad_conv = sum_everywhere(local_grad, ("drift", "beam"))
    return fragment_out, grad_features, grad_conv


def solution(mesh):
    return jax.shard_map(
        body,
        mesh=mesh,
        in_specs=(
            P("drift", None, "beam", None),
            P("drift", "beam", None),
            P("drift", "beam", None),
            P(),
            P(),
            P(),
            P(),
            P(("drift", "beam")),
            P(("drift", "beam")),
            P(("drift", "beam"), None),
        ),
        out_specs=(P(("drift", "beam"), None), P("drift", None, "beam", None), P()),
        check_vma=False,
    )
```

```python
import jax
import jax.numpy as jnp
from jax import lax
from jax.experimental import pallas as pl
from jax.experimental.pallas import tpu as pltpu
from jax.sharding import PartitionSpec as P

BLOCK = 8
REACH = 3
SPARE = 16
DIGIT = 128.0
LIMIT = 56 * 1024 * 1024
bf16 = jnp.bfloat16
f32 = jnp.float32


def contract(left, right, dims):
    return lax.dot_general(left, right, ((dims[0], dims[1]), ((), ())), preferred_element_type=f32)


def plain(left, right):
    return contract(left, right, ((1,), (0,)))


def by_last(left, right):
    return contract(left, right, ((1,), (1,)))


def by_first(left, right):
    return contract(left, right, ((0,), (0,)))


def slope_of(value, sig):
    return sig * (1.0 + value * (1.0 - sig))


def one_hot(index, count):
    places = lax.broadcasted_iota(jnp.int32, (count, index.shape[-1]), 0)
    return jnp.where(places == index, 1.0, 0.0).astype(bf16)


def spread(values, owner, owners):
    parts = [jnp.where(owner == h, values, 0.0).astype(bf16) for h in range(owners)]
    return jnp.concatenate(parts, 0)


def pick(stacked, owner, owners):
    width = stacked.shape[0] // owners
    total = stacked[:width]
    for h in range(1, owners):
        total = jnp.where(owner == h, stacked[h * width : (h + 1) * width], total)
    return total


def store_taps(taps, row, first, tiles):
    count, channels, depth = tiles.shape
    flat = tiles.reshape(count * channels, depth)
    lane = lax.broadcasted_iota(jnp.int32, flat.shape, 1)
    before = jnp.where(lane == 0, 0.0, pltpu.roll(flat, 1, 1))
    after = jnp.where(lane == depth - 1, 0.0, pltpu.roll(flat, depth - 1, 1))
    for place, value in enumerate((before, flat, after)):
        taps[row, first : first + count, place * channels : (place + 1) * channels, :] = (
            value.reshape(count, channels, depth).astype(bf16)
        )


def columns(taps, row, first, count):
    wide = []
    for y in range(first, first + count):
        wide.append(jnp.concatenate([taps[row + a, y] for a in range(REACH)], 0))
    return jnp.concatenate(wide, 1)


def convolve_row(taps, weight, row, height):
    depth = taps.shape[-1]
    channels = weight.shape[0] // REACH
    wide = height * depth
    found = jnp.concatenate(
        [plain(weight, columns(taps, row, y, 2)) for y in range(0, height + REACH - 1, 2)], 1
    )
    total = found[:channels, :wide]
    for b in range(1, REACH):
        part = found[b * channels : (b + 1) * channels, b * depth : b * depth + wide]
        total = total + part
    return total


def forward_kernel(
    feat, x_low, x_high, y_low, y_high, mask, owner, local, weight, taps, slopes, partial, total
):
    rows, channels, height, depth = feat.shape
    owners, _, frag_dev = partial.shape

    def turned(block):
        return jnp.swapaxes(block.astype(f32), 0, 1)

    store_taps(taps, 0, 1, turned(x_low[...]))
    store_taps(taps, rows + 1, 1, turned(x_high[...]))

    def fill(x, _):
        tiles = turned(feat[x])
        live = mask[x]
        gates = [live[:, y * depth : (y + 1) * depth] for y in range(height)]
        gates = jnp.concatenate([jnp.broadcast_to(g, (1, channels, depth)) for g in gates], 0)
        store_taps(taps, x + 1, 1, tiles * gates)
        return 0

    lax.fori_loop(0, rows, fill, 0)

    def edges(x, _):
        store_taps(taps, x, 0, y_low[x].astype(f32)[None])
        store_taps(taps, x, height + 1, y_high[x].astype(f32)[None])
        return 0

    lax.fori_loop(0, rows + 2, edges, 0)
    total[...] = jnp.zeros_like(total)

    def one_row(x, _):
        conv = convolve_row(taps, weight[...], x, height)
        active = jnp.concatenate(
            [taps[x + 1, y + 1, channels : 2 * channels, :] for y in range(height)], 1
        )
        live = mask[x]
        sig = jax.nn.sigmoid(conv)
        hidden = live * (active.astype(f32) + conv * sig)
        slopes[x] = live * slope_of(conv, sig)
        tallies = lax.broadcasted_iota(jnp.int32, (total.shape[0] - owners * channels, 1), 0)
        heads = jnp.where(tallies == owner[x], live, 0.0).astype(bf16)
        rising = jnp.concatenate([spread(hidden, owner[x], owners), heads], 0)
        total[...] += by_last(rising, one_hot(local[x], frag_dev))
        return 0

    lax.fori_loop(0, rows, one_row, 0)
    line = lax.broadcasted_iota(jnp.int32, (SPARE, frag_dev), 0)
    for h in range(owners):
        partial[h, :channels] = total[h * channels : (h + 1) * channels].astype(bf16)
        place = owners * channels + h
        rest = jnp.broadcast_to(total[place : place + 1], (SPARE, frag_dev))
        digits = jnp.zeros_like(rest)
        for d in range(SPARE):
            higher = jnp.floor(rest * (1.0 / DIGIT))
            digits = jnp.where(line == d, rest - higher * DIGIT, digits)
            rest = higher
            if DIGIT ** (d + 1) > rows * height * depth:
                break
        partial[h, channels:] = digits.astype(bf16)


def pool_kernel(parts, pooled, divisor):
    sums = parts[0].astype(f32)
    for h in range(1, parts.shape[0]):
        sums = sums + parts[h].astype(f32)
    channels = pooled.shape[1]
    line = lax.broadcasted_iota(jnp.int32, (SPARE, sums.shape[1]), 0)
    scale = jnp.zeros_like(sums[channels:])
    for d in range(4):
        scale = jnp.where(line == d, DIGIT**d, scale)
    counts = jnp.sum(sums[channels:] * scale, axis=0, keepdims=True)
    below = jnp.maximum(counts, 1.0)
    divisor[...] = jnp.broadcast_to(below, divisor.shape)
    result = (sums[:channels] / below).astype(bf16)
    for h in range(pooled.shape[0]):
        pooled[h] = result


def fragment_kernel(
    table, mine, embed, message, update, cotangent, owner, local, target, out, partial, direct
):
    owners, channels, frag_dev = table.shape
    flat = table[...].reshape(owners * channels, frag_dev)
    from_local = one_hot(local[...], frag_dev)
    source = pick(plain(flat, from_local), owner[...], owners).astype(bf16)
    pre_source = by_first(source, embed[...])
    sig_source = jax.nn.sigmoid(pre_source)
    own_source = (pre_source * sig_source).astype(bf16)
    pre_msg = plain(own_source, message[...])
    sig_msg = jax.nn.sigmoid(pre_msg)
    messages = (pre_msg * sig_msg).astype(bf16)
    to_target = one_hot(target[...], frag_dev)
    gathered = plain(to_target, messages).astype(bf16)
    pre_own = by_first(mine[...], embed[...])
    sig_own = jax.nn.sigmoid(pre_own)
    own = (pre_own * sig_own).astype(bf16)
    out[...] = (own.astype(f32) + plain(gathered, update[...])).astype(bf16)
    back_agg = by_last(cotangent[...], update[...]).astype(bf16)
    back_edge = by_first(to_target, back_agg)
    back_pre = (back_edge * slope_of(pre_msg, sig_msg)).astype(bf16)
    back_source = by_last(back_pre, message[...]) * slope_of(pre_source, sig_source)
    back_pooled = by_last(embed[...], back_source.astype(bf16))
    scattered = by_last(spread(back_pooled, owner[...], owners), from_local)
    partial[...] = scattered.reshape(partial.shape).astype(partial.dtype)
    near = cotangent[...].astype(f32) * slope_of(pre_own, sig_own)
    rough = near.astype(bf16)
    rest = (near - rough.astype(f32)).astype(bf16)
    direct[...] = by_last(embed[...], rough) + by_last(embed[...], rest)


def mean_kernel(parts, direct, divisor, mean):
    total = direct[...]
    for h in range(parts.shape[0]):
        total = total + parts[h].astype(f32)
    result = (total / divisor[:1]).astype(bf16)
    for h in range(mean.shape[0]):
        mean[h] = result


def hidden_kernel(table, owner, local, mask, slopes, back_hidden, back_conv):
    owners, channels, frag_dev = table.shape
    rows, height, _, depth = back_conv.shape
    flat = table[...].reshape(owners * channels, frag_dev)

    def one_row(x, _):
        found = plain(flat, one_hot(local[x], frag_dev))
        hidden = pick(found, owner[x], owners)
        back_hidden[x] = mask[x] * hidden
        grad = (hidden * slopes[x]).astype(bf16)
        for y in range(height):
            back_conv[x, y] = grad[:, y * depth : (y + 1) * depth]
        return 0

    lax.fori_loop(0, rows, one_row, 0)


def weight_kernel(taps, back_conv, grad):
    rows, height, channels, depth = back_conv.shape
    empty = jnp.zeros((channels, depth), bf16)
    grad[...] = jnp.zeros_like(grad)

    def one_row(x, _):
        slabs = [back_conv[x, y] for y in range(height)]
        lines = []
        for b in range(REACH):
            lines.append(jnp.concatenate([empty] * b + slabs + [empty] * (REACH - 1 - b), 1))
        stacked = jnp.concatenate(lines, 0)
        total = None
        for y in range(0, height + REACH - 1, 2):
            term = by_last(stacked[:, y * depth : (y + 2) * depth], columns(taps, x, y, 2))
            total = term if total is None else total + term
        grad[...] += total
        return 0

    lax.fori_loop(0, rows, one_row, 0)


def backward_kernel(
    back_conv, x_low, x_high, y_low, y_high, back_hidden, mask, weight, grad, taps
):
    rows, height, channels, depth = back_conv.shape
    store_taps(taps, 0, 1, x_low[...].astype(f32))
    store_taps(taps, rows + 1, 1, x_high[...].astype(f32))

    def fill(x, _):
        store_taps(taps, x + 1, 1, back_conv[x].astype(f32))
        return 0

    lax.fori_loop(0, rows, fill, 0)

    def edges(x, _):
        store_taps(taps, x, 0, y_low[x].astype(f32)[None])
        store_taps(taps, x, height + 1, y_high[x].astype(f32)[None])
        return 0

    lax.fori_loop(0, rows + 2, edges, 0)

    def one_row(x, _):
        result = mask[x] * (back_hidden[x] + convolve_row(taps, weight[...], x, height))
        tiles = [result[:, y * depth : (y + 1) * depth][None] for y in range(height)]
        grad[x] = jnp.swapaxes(jnp.concatenate(tiles, 0), 0, 1)
        return 0

    lax.fori_loop(0, rows, one_row, 0)


def call(kernel, shapes, *operands, scratch=(), micros=2):
    return pl.pallas_call(
        kernel,
        out_shape=[jax.ShapeDtypeStruct(shape, kind) for shape, kind in shapes],
        scratch_shapes=list(scratch),
        cost_estimate=pl.CostEstimate(
            flops=micros * 10**9, bytes_accessed=micros * 3 * 10**6, transcendentals=0
        ),
        compiler_params=pltpu.CompilerParams(vmem_limit_bytes=LIMIT),
    )(*operands)


def pass_on(low, high, axis):
    count = lax.axis_size(axis)
    up = [(i, i + 1) for i in range(count - 1)]
    down = [(i + 1, i) for i in range(count - 1)]
    return lax.ppermute(high, axis, up), lax.ppermute(low, axis, down)


def exchange(parts, axes):
    return lax.all_to_all(parts, axes, 0, 0, tiled=True)


def sum_everywhere(values, axes):
    count = lax.axis_size(axes)
    flat = values.reshape(-1)
    share = -(-flat.shape[0] // count)
    flat = jnp.pad(flat, (0, share * count - flat.shape[0])).reshape(count, share)
    mine = exchange(flat, axes).sum(0)
    back = exchange(jnp.broadcast_to(mine[None], flat.shape), axes)
    return back.reshape(-1)[: values.size].reshape(values.shape)


def body(
    features,
    occupied,
    voxel_fragment,
    conv_weight,
    embed_weight,
    message_weight,
    update_weight,
    edge_source,
    edge_target,
    out_cotangent,
):
    rows, channels, height, depth = features.shape
    frag_dev, hid = out_cotangent.shape
    owners = lax.axis_size("beam")
    edge_count = edge_source.shape[0]
    plane = height * depth
    mask = jnp.repeat(jnp.repeat(jnp.repeat(occupied, BLOCK, 0), BLOCK, 1), BLOCK, 2)
    gate = mask.astype(bf16)

    split = conv_weight.reshape(channels, REACH, REACH, REACH, channels)
    stacked_shape = (REACH * channels, REACH * REACH * channels)
    stacked = split.transpose(2, 0, 1, 3, 4).reshape(stacked_shape)
    flipped = split[:, ::-1, ::-1, ::-1].transpose(2, 4, 1, 3, 0).reshape(stacked_shape)

    x_low, x_high = pass_on(
        features[0] * gate[0][None], features[-1] * gate[-1][None], "drift"
    )
    ends = []
    for y in (0, height - 1):
        side = features[:, :, y] * gate[:, None, y]
        ends.append(jnp.concatenate([x_low[None, :, y], side, x_high[None, :, y]], 0))
    y_low, y_high = pass_on(ends[0], ends[1], "beam")

    live = mask.astype(f32).reshape(rows, 1, plane)
    owner = (voxel_fragment // frag_dev).reshape(rows, 1, plane)
    local = (voxel_fragment % frag_dev).reshape(rows, 1, plane)
    heads = -(-owners // 16) * 16
    padded = (rows + 2, height + 2, REACH * channels, depth)
    taps, slopes, partial = call(
        forward_kernel,
        [
            (padded, bf16),
            ((rows, channels, plane), f32),
            ((owners, channels + SPARE, frag_dev), bf16),
        ],
        features, x_low, x_high, y_low, y_high, live, owner, local, stacked, micros=12,
        scratch=[pltpu.VMEM((owners * channels + heads, frag_dev), f32)],
    )
    spread_shape = (owners, channels, frag_dev)
    pooled, divisor = call(
        pool_kernel,
        [(spread_shape, bf16), ((8, frag_dev), f32)],
        exchange(partial, "beam"),
    )
    table = exchange(pooled, "beam")
    fragment_out, back_parts, direct = call(
        fragment_kernel,
        [((frag_dev, hid), bf16), (spread_shape, bf16), ((channels, frag_dev), f32)],
        table, pooled[0], embed_weight, message_weight, update_weight, out_cotangent,
        (edge_source // frag_dev).reshape(1, edge_count),
        (edge_source % frag_dev).reshape(1, edge_count),
        edge_target.reshape(1, edge_count),
    )
    (mean,) = call(
        mean_kernel, [(spread_shape, bf16)], exchange(back_parts, "beam"), direct, divisor
    )
    back_hidden, back_conv = call(
        hidden_kernel,
        [((rows, channels, plane), f32), ((rows, height, channels, depth), bf16)],
        exchange(mean, "beam"), owner, local, live, slopes, micros=7,
    )
    gx_low, gx_high = pass_on(back_conv[0], back_conv[-1], "drift")
    ends = [
        jnp.concatenate([gx_low[None, y], back_conv[:, y], gx_high[None, y]], 0)
        for y in (0, height - 1)
    ]
    gy_low, gy_high = pass_on(ends[0], ends[1], "beam")
    (stacked_grad,) = call(weight_kernel, [(stacked_shape, f32)], taps, back_conv, micros=8)
    (grad_features,) = call(
        backward_kernel,
        [(features.shape, f32)],
        back_conv, gx_low, gx_high, gy_low, gy_high, back_hidden, live, flipped, micros=10,
        scratch=[pltpu.VMEM(padded, bf16)],
    )
    grad_conv = (
        sum_everywhere(stacked_grad, ("drift", "beam"))
        .reshape(REACH, channels, REACH, REACH, channels)
        .transpose(1, 2, 0, 3, 4)
        .reshape(conv_weight.shape)
    )
    return fragment_out, grad_features, grad_conv


def solution(mesh):
    return jax.shard_map(
        body,
        mesh=mesh,
        in_specs=(
            P("drift", None, "beam", None),
            P("drift", "beam", None),
            P("drift", "beam", None),
            P(),
            P(),
            P(),
            P(),
            P(("drift", "beam")),
            P(("drift", "beam")),
            P(("drift", "beam"), None),
        ),
        out_specs=(P(("drift", "beam"), None), P("drift", None, "beam", None), P()),
        check_vma=False,
    )
```

```python
import functools

import jax
import jax.numpy as jnp
from jax import lax
from jax.experimental import pallas as pl
from jax.experimental.pallas import tpu as pltpu
from jax.sharding import PartitionSpec as P

BLOCK = 8
REACH = 3
SPARE = 16
LANES = 128
SUBLANES = 8
DIGIT = 128.0
LIMIT = 56 * 1024 * 1024
bf16 = jnp.bfloat16
f32 = jnp.float32


def contract(left, right, dims):
    return lax.dot_general(left, right, ((dims[0], dims[1]), ((), ())), preferred_element_type=f32)


def plain(left, right):
    return contract(left, right, ((1,), (0,)))


def by_last(left, right):
    return contract(left, right, ((1,), (1,)))


def by_first(left, right):
    return contract(left, right, ((0,), (0,)))


def slope_of(value, sig):
    return sig * (1.0 + value * (1.0 - sig))


def line_of(block):
    return jnp.concatenate([block[y : y + 1] for y in range(block.shape[0])], 1)


def live_line(lanes, row, height):
    bands = lanes[row // BLOCK]
    return jnp.concatenate([bands[y // BLOCK : y // BLOCK + 1] for y in range(height)], 1)


def owner_and_local(index, size):
    if size & (size - 1) == 0:
        return index >> (size.bit_length() - 1), index & (size - 1)
    return index // size, index % size


def one_hot(index, count):
    places = lax.broadcasted_iota(jnp.int32, (count, index.shape[-1]), 0)
    return jnp.where(places == index, 1.0, 0.0).astype(bf16)


def spread(values, owner, owners):
    parts = [jnp.where(owner == h, values, 0.0).astype(bf16) for h in range(owners)]
    return jnp.concatenate(parts, 0)


def pick(stacked, owner, owners):
    width = stacked.shape[0] // owners
    total = stacked[:width]
    for h in range(1, owners):
        total = jnp.where(owner == h, stacked[h * width : (h + 1) * width], total)
    return total


def store_taps(taps, row, first, tiles):
    count, channels, depth = tiles.shape
    flat = tiles.reshape(count * channels, depth)
    lane = lax.broadcasted_iota(jnp.int32, (1, depth), 1)
    after_first = jnp.where(lane == 0, 0.0, 1.0).astype(bf16)
    before_last = jnp.where(lane == depth - 1, 0.0, 1.0).astype(bf16)
    before = pltpu.roll(flat, 1, 1) * after_first
    after = pltpu.roll(flat, depth - 1, 1) * before_last
    for place, value in enumerate((before, flat, after)):
        taps[row, first : first + count, place * channels : (place + 1) * channels, :] = (
            value.reshape(count, channels, depth)
        )


def row_copy(source, target, arrived):
    return lambda x: pltpu.make_async_copy(source.at[x], target.at[x], arrived.at[x])


def start_rows(copy, rows):
    def step(x, _):
        copy(x).start()
        return 0

    lax.fori_loop(0, rows, step, 0)


def wait_rows(copy, rows):
    def step(x, _):
        copy(x).wait()
        return 0

    lax.fori_loop(0, rows, step, 0)


def columns(taps, row, first, count):
    wide = []
    for y in range(first, first + count):
        wide.append(jnp.concatenate([taps[row + a, y] for a in range(REACH)], 0))
    return jnp.concatenate(wide, 1)


def convolve_row(taps, weight, row, height):
    depth = taps.shape[-1]
    channels = weight.shape[0] // REACH
    wide = height * depth
    found = jnp.concatenate(
        [plain(weight, columns(taps, row, y, 2)) for y in range(0, height + REACH - 1, 2)], 1
    )
    total = found[:channels, :wide]
    for b in range(1, REACH):
        part = found[b * channels : (b + 1) * channels, b * depth : b * depth + wide]
        total = total + part
    return total


def forward_kernel(
    feat, x_low, x_high, y_low, y_high, lanes, fragment, weight, taps_out, slopes_out, partial,
    taps, slopes, total, taps_sent, slopes_sent
):
    rows, channels, height, depth = feat.shape
    owners, _, frag_dev = partial.shape

    def turned(block):
        return jnp.swapaxes(block.astype(f32), 0, 1)

    send_taps = row_copy(taps, taps_out, taps_sent)
    send_slopes = row_copy(slopes, slopes_out, slopes_sent)

    store_taps(taps, 0, 1, turned(x_low[...]).astype(bf16))
    store_taps(taps, rows + 1, 1, turned(x_high[...]).astype(bf16))

    def fill(x, _):
        tiles = turned(feat[x])
        live = live_line(lanes, x, height)
        gates = [live[:, y * depth : (y + 1) * depth] for y in range(height)]
        gates = jnp.concatenate([jnp.broadcast_to(g, (1, channels, depth)) for g in gates], 0)
        store_taps(taps, x + 1, 1, (tiles * gates).astype(bf16))
        return 0

    lax.fori_loop(0, rows, fill, 0)

    def edges(x, _):
        store_taps(taps, x, 0, y_low[x][None])
        store_taps(taps, x, height + 1, y_high[x][None])
        return 0

    lax.fori_loop(0, rows + 2, edges, 0)
    start_rows(send_taps, rows + 2)
    total[...] = jnp.zeros_like(total)

    def one_row(x, _):
        conv = convolve_row(taps, weight[...], x, height)
        active = jnp.concatenate(
            [taps[x + 1, y + 1, channels : 2 * channels, :] for y in range(height)], 1
        )
        live = live_line(lanes, x, height)
        owner, local = owner_and_local(line_of(fragment[x]), frag_dev)
        sig = jax.nn.sigmoid(conv)
        hidden = live * (active.astype(f32) + conv * sig)
        slopes[x] = (live * slope_of(conv, sig)).astype(bf16)
        send_slopes(x).start()
        tallies = lax.broadcasted_iota(jnp.int32, (total.shape[0] - owners * channels, 1), 0)
        heads = jnp.where(tallies == owner, live, 0.0).astype(bf16)
        rising = jnp.concatenate([spread(hidden, owner, owners), heads], 0)
        total[...] += by_last(rising, one_hot(local, frag_dev))
        return 0

    lax.fori_loop(0, rows, one_row, 0)
    line = lax.broadcasted_iota(jnp.int32, (SPARE, frag_dev), 0)
    for h in range(owners):
        partial[h, :channels] = total[h * channels : (h + 1) * channels].astype(bf16)
        place = owners * channels + h
        rest = jnp.broadcast_to(total[place : place + 1], (SPARE, frag_dev))
        digits = jnp.zeros_like(rest)
        for d in range(SPARE):
            higher = jnp.floor(rest * (1.0 / DIGIT))
            digits = jnp.where(line == d, rest - higher * DIGIT, digits)
            rest = higher
            if DIGIT ** (d + 1) > rows * height * depth:
                break
        partial[h, channels:] = digits.astype(bf16)
    wait_rows(send_taps, rows + 2)
    wait_rows(send_slopes, rows)


def pool_kernel(parts, pooled, divisor):
    sums = parts[0].astype(f32)
    for h in range(1, parts.shape[0]):
        sums = sums + parts[h].astype(f32)
    channels = pooled.shape[1]
    line = lax.broadcasted_iota(jnp.int32, (SPARE, sums.shape[1]), 0)
    scale = jnp.zeros_like(sums[channels:])
    for d in range(4):
        scale = jnp.where(line == d, DIGIT**d, scale)
    counts = jnp.sum(sums[channels:] * scale, axis=0, keepdims=True)
    below = jnp.maximum(counts, 1.0)
    divisor[...] = jnp.broadcast_to(below, divisor.shape)
    result = (sums[:channels] / below).astype(bf16)
    for h in range(pooled.shape[0]):
        pooled[h] = result


def fragment_kernel(
    table, mine, embed, message, update, cotangent, edge_from, target, out, partial, direct
):
    owners, channels, frag_dev = table.shape
    flat = table[...].reshape(owners * channels, frag_dev)
    owner, local = owner_and_local(edge_from[...], frag_dev)
    from_local = one_hot(local, frag_dev)
    source = pick(plain(flat, from_local), owner, owners).astype(bf16)
    pre_source = by_first(source, embed[...])
    sig_source = jax.nn.sigmoid(pre_source)
    own_source = (pre_source * sig_source).astype(bf16)
    pre_msg = plain(own_source, message[...])
    sig_msg = jax.nn.sigmoid(pre_msg)
    messages = (pre_msg * sig_msg).astype(bf16)
    to_target = one_hot(target[...], frag_dev)
    gathered = plain(to_target, messages).astype(bf16)
    pre_own = by_first(mine[...], embed[...])
    sig_own = jax.nn.sigmoid(pre_own)
    own = (pre_own * sig_own).astype(bf16)
    out[...] = (own.astype(f32) + plain(gathered, update[...])).astype(bf16)
    back_agg = by_last(cotangent[...], update[...]).astype(bf16)
    back_edge = by_first(to_target, back_agg)
    back_pre = (back_edge * slope_of(pre_msg, sig_msg)).astype(bf16)
    back_source = by_last(back_pre, message[...]) * slope_of(pre_source, sig_source)
    back_pooled = by_last(embed[...], back_source.astype(bf16))
    scattered = by_last(spread(back_pooled, owner, owners), from_local)
    partial[...] = scattered.reshape(partial.shape).astype(partial.dtype)
    near = cotangent[...].astype(f32) * slope_of(pre_own, sig_own)
    rough = near.astype(bf16)
    rest = (near - rough.astype(f32)).astype(bf16)
    direct[...] = by_last(embed[...], rough) + by_last(embed[...], rest)


def mean_kernel(parts, direct, divisor, mean):
    total = direct[...]
    for h in range(parts.shape[0]):
        total = total + parts[h].astype(f32)
    result = (total / divisor[:1]).astype(bf16)
    for h in range(mean.shape[0]):
        mean[h] = result


def hidden_kernel(
    table, fragment, lanes, slopes_in, hidden_out, conv_out,
    slopes, back_hidden, back_conv, slopes_here, hidden_sent, conv_sent
):
    owners, channels, frag_dev = table.shape
    rows, height, _, depth = back_conv.shape
    flat = table[...].reshape(owners * channels, frag_dev)
    fetch = row_copy(slopes_in, slopes, slopes_here)
    send_hidden = row_copy(back_hidden, hidden_out, hidden_sent)
    send_conv = row_copy(back_conv, conv_out, conv_sent)
    start_rows(fetch, rows)

    def one_row(x, _):
        owner, local = owner_and_local(line_of(fragment[x]), frag_dev)
        found = plain(flat, one_hot(local, frag_dev))
        hidden = pick(found, owner, owners)
        back_hidden[x] = (live_line(lanes, x, height) * hidden).astype(bf16)
        send_hidden(x).start()
        fetch(x).wait()
        grad = (hidden * slopes[x].astype(f32)).astype(bf16)
        for y in range(height):
            back_conv[x, y] = grad[:, y * depth : (y + 1) * depth]
        send_conv(x).start()
        return 0

    lax.fori_loop(0, rows, one_row, 0)
    wait_rows(send_hidden, rows)
    wait_rows(send_conv, rows)


def weight_kernel(taps, back_conv, packed, grad, near, arrived):
    rows, height, channels, depth = back_conv.shape
    empty = jnp.zeros((channels, depth), bf16)
    grad[...] = jnp.zeros_like(grad)

    def fetch(x):
        return pltpu.make_async_copy(taps.at[x], near.at[x], arrived.at[x])

    for x in range(rows + REACH - 1):
        fetch(x).start()
    for x in range(REACH - 1):
        fetch(x).wait()

    def one_row(x, _):
        fetch(x + REACH - 1).wait()
        slabs = [back_conv[x, y] for y in range(height)]
        lines = []
        for b in range(REACH):
            lines.append(jnp.concatenate([empty] * b + slabs + [empty] * (REACH - 1 - b), 1))
        stacked = jnp.concatenate(lines, 0)
        total = None
        for y in range(0, height + REACH - 1, 2):
            term = by_last(stacked[:, y * depth : (y + 2) * depth], columns(near, x, y, 2))
            total = term if total is None else total + term
        grad[...] += total
        return 0

    lax.fori_loop(0, rows, one_row, 0)
    packed[...] = jnp.zeros_like(packed)
    for place, part in packed_parts(grad.shape):
        height = part[0].stop - part[0].start
        width = part[1].stop - part[1].start
        packed[place[0] : place[0] + height, place[1] : place[1] + width] = grad[part]


def packed_parts(shape):
    height, width = shape
    full = width // LANES * LANES
    rest = width - full
    parts = []
    for left in range(0, full, LANES):
        parts.append(((left // LANES * height, 0), (slice(0, height), slice(left, left + LANES))))
    if rest:
        folds = LANES // rest
        step = height // folds
        for k in range(folds):
            source = (slice(k * step, (k + 1) * step), slice(full, width))
            parts.append(((full // LANES * height, k * rest), source))
    return parts


def unpack(packed, shape):
    height, width = shape
    full = width // LANES * LANES
    rest = width - full
    blocks = [packed[left // LANES * height :][:height] for left in range(0, full, LANES)]
    if rest:
        folds = LANES // rest
        step = height // folds
        tail = packed[full // LANES * height :][:step]
        blocks.append(tail.reshape(step, folds, rest).swapaxes(0, 1).reshape(height, rest))
    return jnp.concatenate(blocks, 1)


def weight_call(taps, back_conv, shape, lines):
    whole = pl.BlockSpec(memory_space=pltpu.VMEM)
    return pl.pallas_call(
        weight_kernel,
        in_specs=[pl.BlockSpec(memory_space=pl.ANY), whole],
        out_specs=whole,
        out_shape=jax.ShapeDtypeStruct((lines, LANES), f32),
        scratch_shapes=[pltpu.VMEM(shape, f32), pltpu.VMEM(taps.shape, bf16), pltpu.SemaphoreType.DMA((taps.shape[0],))],
        cost_estimate=cost(8),
        compiler_params=pltpu.CompilerParams(vmem_limit_bytes=LIMIT),
    )(taps, back_conv)


def backward_kernel(
    back_conv, x_low, x_high, y_low, y_high, back_hidden, lanes, weight, grad_out,
    grad, taps, sent
):
    rows, height, channels, depth = back_conv.shape
    send = row_copy(grad, grad_out, sent)
    store_taps(taps, 0, 1, x_low[...])
    store_taps(taps, rows + 1, 1, x_high[...])

    def fill(x, _):
        store_taps(taps, x + 1, 1, back_conv[x])
        return 0

    lax.fori_loop(0, rows, fill, 0)

    def edges(x, _):
        store_taps(taps, x, 0, y_low[x][None])
        store_taps(taps, x, height + 1, y_high[x][None])
        return 0

    lax.fori_loop(0, rows + REACH - 1, edges, 0)

    def one_row(x, _):
        live = live_line(lanes, x, height)
        result = live * (back_hidden[x].astype(f32) + convolve_row(taps, weight[...], x, height))
        tiles = [result[:, y * depth : (y + 1) * depth][None] for y in range(height)]
        grad[x] = jnp.swapaxes(jnp.concatenate(tiles, 0), 0, 1)
        send(x).start()
        return 0

    lax.fori_loop(0, rows, one_row, 0)
    wait_rows(send, rows)


def cost(micros):
    return pl.CostEstimate(
        flops=micros * 10**9, bytes_accessed=micros * 3 * 10**6, transcendentals=0
    )


def call(kernel, shapes, *operands, scratch=(), micros=2, far_in=(), far_out=()):
    here, there = pl.BlockSpec(memory_space=pltpu.VMEM), pl.BlockSpec(memory_space=pl.ANY)
    return pl.pallas_call(
        kernel,
        in_specs=[there if i in far_in else here for i in range(len(operands))],
        out_specs=[there if i in far_out else here for i in range(len(shapes))],
        out_shape=[jax.ShapeDtypeStruct(shape, kind) for shape, kind in shapes],
        scratch_shapes=list(scratch),
        cost_estimate=cost(micros),
        compiler_params=pltpu.CompilerParams(vmem_limit_bytes=LIMIT),
    )(*operands)


def pass_on(low, high, axis):
    count = lax.axis_size(axis)
    up = [(i, i + 1) for i in range(count - 1)]
    down = [(i + 1, i) for i in range(count - 1)]
    return lax.ppermute(high, axis, up), lax.ppermute(low, axis, down)


def exchange(parts, axes):
    return lax.all_to_all(parts, axes, 0, 0, tiled=True)


def body(
    features,
    occupied,
    voxel_fragment,
    conv_weight,
    embed_weight,
    message_weight,
    update_weight,
    edge_source,
    edge_target,
    out_cotangent,
):
    rows, channels, height, depth = features.shape
    frag_dev, hid = out_cotangent.shape
    owners = lax.axis_size("beam")
    edge_count = edge_source.shape[0]
    plane = height * depth
    lanes = jnp.repeat(occupied, BLOCK, 2).astype(f32)
    gate = jnp.repeat(jnp.repeat(lanes, BLOCK, 0), BLOCK, 1).astype(bf16)

    split = conv_weight.reshape(channels, REACH, REACH, REACH, channels)
    stacked_shape = (REACH * channels, REACH * REACH * channels)
    stacked = split.transpose(2, 0, 1, 3, 4).reshape(stacked_shape)
    flipped = split[:, ::-1, ::-1, ::-1].transpose(2, 4, 1, 3, 0).reshape(stacked_shape)

    x_low, x_high = pass_on(
        features[0] * gate[0][None], features[-1] * gate[-1][None], "drift"
    )
    ends = []
    for y in (0, height - 1):
        side = features[:, :, y] * gate[:, None, y]
        ends.append(jnp.concatenate([x_low[None, :, y], side, x_high[None, :, y]], 0))
    y_low, y_high = pass_on(ends[0], ends[1], "beam")

    heads = -(-owners // 16) * 16
    line_shape = (rows, channels, plane)
    conv_shape = (rows, height, channels, depth)
    dma = lambda count: pltpu.SemaphoreType.DMA((count,))
    padded = (rows + 2, height + 2, REACH * channels, depth)
    taps, slopes, partial = call(
        forward_kernel,
        [
            (padded, bf16),
            (line_shape, bf16),
            ((owners, channels + SPARE, frag_dev), bf16),
        ],
        features, x_low, x_high, y_low, y_high, lanes, voxel_fragment, stacked, micros=12,
        scratch=[
            pltpu.VMEM(padded, bf16), pltpu.VMEM(line_shape, bf16),
            pltpu.VMEM((owners * channels + heads, frag_dev), f32), dma(rows + 2), dma(rows),
        ],
        far_out=(0, 1),
    )
    spread_shape = (owners, channels, frag_dev)
    pooled, divisor = call(
        pool_kernel,
        [(spread_shape, bf16), ((8, frag_dev), f32)],
        exchange(partial, "beam"),
    )
    table = exchange(pooled, "beam")
    fragment_out, back_parts, direct = call(
        fragment_kernel,
        [((frag_dev, hid), bf16), (spread_shape, bf16), ((channels, frag_dev), f32)],
        table, pooled[0], embed_weight, message_weight, update_weight, out_cotangent,
        edge_source.reshape(1, edge_count),
        edge_target.reshape(1, edge_count),
    )
    (mean,) = call(
        mean_kernel, [(spread_shape, bf16)], exchange(back_parts, "beam"), direct, divisor
    )
    back_hidden, back_conv = call(
        hidden_kernel,
        [(line_shape, bf16), (conv_shape, bf16)],
        exchange(mean, "beam"), voxel_fragment, lanes, slopes, micros=7,
        scratch=[
            pltpu.VMEM(line_shape, bf16), pltpu.VMEM(line_shape, bf16),
            pltpu.VMEM(conv_shape, bf16), dma(rows), dma(rows), dma(rows),
        ],
        far_in=(3,), far_out=(0, 1),
    )
    gx_low, gx_high = pass_on(back_conv[0], back_conv[-1], "drift")
    everyone = ("drift", "beam")
    devices = lax.axis_size(everyone)
    tile = SUBLANES * LANES
    share = -(-conv_weight.size // (devices * tile)) * SUBLANES
    packed = weight_call(taps, back_conv, stacked_shape, devices * share)
    ends = [
        jnp.concatenate([gx_low[None, y], back_conv[:, y], gx_high[None, y]], 0)
        for y in (0, height - 1)
    ]
    gy_low, gy_high = pass_on(ends[0], ends[1], "beam")
    (grad_features,) = call(
        backward_kernel,
        [(features.shape, f32)],
        back_conv, gx_low, gx_high, gy_low, gy_high, back_hidden, lanes, flipped, micros=10,
        scratch=[pltpu.VMEM(features.shape, f32), pltpu.VMEM(padded, bf16), dma(rows)],
        far_out=(0,),
    )
    parts = exchange(packed, everyone).reshape(devices, share, LANES)
    full = exchange(jnp.broadcast_to(parts.sum(0)[None], parts.shape), everyone)
    grad_conv = (
        unpack(full.reshape(devices * share, LANES), stacked_shape)
        .reshape(REACH, channels, REACH, REACH, channels)
        .transpose(1, 2, 0, 3, 4)
        .reshape(conv_weight.shape)
    )
    return fragment_out, grad_features, grad_conv


def solution(mesh):
    return jax.shard_map(
        body,
        mesh=mesh,
        in_specs=(
            P("drift", None, "beam", None),
            P("drift", "beam", None),
            P("drift", "beam", None),
            P(),
            P(),
            P(),
            P(),
            P(("drift", "beam")),
            P(("drift", "beam")),
            P(("drift", "beam"), None),
        ),
        out_specs=(P(("drift", "beam"), None), P("drift", None, "beam", None), P()),
        check_vma=False,
    )
```

```python
import functools

import jax
import jax.numpy as jnp
from jax import lax
from jax.experimental import pallas as pl
from jax.experimental.pallas import tpu as pltpu
from jax.sharding import PartitionSpec as P

BLOCK = 8
REACH = 3
RIM = 2
SPARE = 16
LANES = 128
SUBLANES = 8
DIGIT = 128.0
LIMIT = 56 * 1024 * 1024
bf16 = jnp.bfloat16
f32 = jnp.float32


def contract(left, right, dims):
    return lax.dot_general(left, right, ((dims[0], dims[1]), ((), ())), preferred_element_type=f32)


def plain(left, right):
    return contract(left, right, ((1,), (0,)))


def by_last(left, right):
    return contract(left, right, ((1,), (1,)))


def by_first(left, right):
    return contract(left, right, ((0,), (0,)))


def slope_of(value, sig):
    return sig * (1.0 + value * (1.0 - sig))


def line_of(block):
    return jnp.concatenate([block[y : y + 1] for y in range(block.shape[0])], 1)


def live_line(lanes, row, height):
    bands = lanes[row // BLOCK]
    return jnp.concatenate([bands[y // BLOCK : y // BLOCK + 1] for y in range(height)], 1)


def with_rims(line, sides, place):
    return jnp.concatenate([sides[0, pl.ds(place, 1)], line, sides[1, pl.ds(place, 1)]], 1)


def owner_and_local(index, size):
    if size & (size - 1) == 0:
        return index >> (size.bit_length() - 1), index & (size - 1)
    return index // size, index % size


def one_hot(index, count):
    places = lax.broadcasted_iota(jnp.int32, (count, index.shape[-1]), 0)
    return jnp.where(places == index, 1.0, 0.0).astype(bf16)


def spread(values, owner, owners):
    parts = [jnp.where(owner == h, values, 0.0).astype(bf16) for h in range(owners)]
    return jnp.concatenate(parts, 0)


def pick(stacked, owner, owners):
    width = stacked.shape[0] // owners
    total = stacked[:width]
    for h in range(1, owners):
        total = jnp.where(owner == h, stacked[h * width : (h + 1) * width], total)
    return total


def store_taps(taps, row, first, tiles):
    count, channels, depth = tiles.shape
    flat = tiles.reshape(count * channels, depth)
    lane = lax.broadcasted_iota(jnp.int32, (1, depth), 1)
    after_first = jnp.where(lane == 0, 0.0, 1.0).astype(bf16)
    before_last = jnp.where(lane == depth - 1, 0.0, 1.0).astype(bf16)
    before = pltpu.roll(flat, 1, 1) * after_first
    after = pltpu.roll(flat, depth - 1, 1) * before_last
    for place, value in enumerate((before, flat, after)):
        taps[row, first : first + count, place * channels : (place + 1) * channels, :] = (
            value.reshape(count, channels, depth)
        )


def row_copy(source, target, arrived):
    return lambda x: pltpu.make_async_copy(source.at[x], target.at[x], arrived.at[x])


def start_rows(copy, rows):
    def step(x, _):
        copy(x).start()
        return 0

    lax.fori_loop(0, rows, step, 0)


def wait_rows(copy, rows):
    def step(x, _):
        copy(x).wait()
        return 0

    lax.fori_loop(0, rows, step, 0)


def columns(taps, row, first, count):
    wide = []
    for y in range(first, first + count):
        wide.append(jnp.concatenate([taps[row + a, y] for a in range(REACH)], 0))
    return jnp.concatenate(wide, 1)


def convolve_row(taps, weight, row, height):
    depth = taps.shape[-1]
    channels = weight.shape[0] // REACH
    wide = height * depth
    found = jnp.concatenate(
        [plain(weight, columns(taps, row, y, 2)) for y in range(0, height + REACH - 1, 2)], 1
    )
    total = found[:channels, :wide]
    for b in range(1, REACH):
        part = found[b * channels : (b + 1) * channels, b * depth : b * depth + wide]
        total = total + part
    return total


def forward_kernel(
    feat, x_low, x_high, y_low, y_high, lanes, fragment, weight, taps_out, slopes_out, partial,
    sides, taps, slopes, total, rims, taps_sent, slopes_sent, rims_here
):
    rows, channels, height, depth = feat.shape
    owners, _, frag_dev = partial.shape

    def turned(block):
        return jnp.swapaxes(block.astype(f32), 0, 1)

    send_taps = row_copy(taps, taps_out, taps_sent)
    send_slopes = row_copy(slopes, slopes_out, slopes_sent)

    get_low = pltpu.make_async_copy(y_low, rims.at[0], rims_here.at[0])
    get_high = pltpu.make_async_copy(y_high, rims.at[1], rims_here.at[1])
    get_low.start()
    get_high.start()
    store_taps(taps, 0, RIM, turned(x_low[...]).astype(bf16))
    store_taps(taps, rows + 1, RIM, turned(x_high[...]).astype(bf16))

    def fill(x, _):
        tiles = turned(feat[x])
        live = live_line(lanes, x, height)
        gates = [live[:, y * depth : (y + 1) * depth] for y in range(height)]
        gates = jnp.concatenate([jnp.broadcast_to(g, (1, channels, depth)) for g in gates], 0)
        store_taps(taps, x + 1, RIM, (tiles * gates).astype(bf16))
        return 0

    lax.fori_loop(0, rows, fill, 0)
    get_low.wait()
    get_high.wait()

    def edges(x, _):
        store_taps(taps, x, 0, rims[0, pl.ds(RIM * x, RIM)])
        store_taps(taps, x, height + RIM, rims[1, pl.ds(RIM * x, RIM)])
        return 0

    lax.fori_loop(0, rows + 2, edges, 0)
    for side in range(2):
        sides[side] = rims[side, RIM * (rows + 2)].astype(f32)
    start_rows(send_taps, rows + 2)
    total[...] = jnp.zeros_like(total)

    def one_row(x, _):
        wide = convolve_row(taps, weight[...], x, height + 2)
        active = jnp.concatenate(
            [taps[x + 1, y + RIM, channels : 2 * channels, :] for y in range(height)], 1
        )
        live = live_line(lanes, x, height)
        owner, local = owner_and_local(line_of(fragment[x]), frag_dev)
        sig = jax.nn.sigmoid(wide)
        slopes[x] = (with_rims(live, sides, 2 * rows + x) * slope_of(wide, sig)).astype(bf16)
        send_slopes(x).start()
        inner = slice(depth, depth + height * depth)
        conv = wide[:, inner]
        hidden = live * (active.astype(f32) + conv * sig[:, inner])
        tallies = lax.broadcasted_iota(jnp.int32, (total.shape[0] - owners * channels, 1), 0)
        heads = jnp.where(tallies == owner, live, 0.0).astype(bf16)
        rising = jnp.concatenate([spread(hidden, owner, owners), heads], 0)
        total[...] += by_last(rising, one_hot(local, frag_dev))
        return 0

    lax.fori_loop(0, rows, one_row, 0)
    line = lax.broadcasted_iota(jnp.int32, (SPARE, frag_dev), 0)
    for h in range(owners):
        partial[h, :channels] = total[h * channels : (h + 1) * channels].astype(bf16)
        place = owners * channels + h
        rest = jnp.broadcast_to(total[place : place + 1], (SPARE, frag_dev))
        digits = jnp.zeros_like(rest)
        for d in range(SPARE):
            higher = jnp.floor(rest * (1.0 / DIGIT))
            digits = jnp.where(line == d, rest - higher * DIGIT, digits)
            rest = higher
            if DIGIT ** (d + 1) > rows * height * depth:
                break
        partial[h, channels:] = digits.astype(bf16)
    wait_rows(send_taps, rows + 2)
    wait_rows(send_slopes, rows)


def pool_kernel(parts, pooled, divisor):
    sums = parts[0].astype(f32)
    for h in range(1, parts.shape[0]):
        sums = sums + parts[h].astype(f32)
    channels = pooled.shape[1]
    line = lax.broadcasted_iota(jnp.int32, (SPARE, sums.shape[1]), 0)
    scale = jnp.zeros_like(sums[channels:])
    for d in range(4):
        scale = jnp.where(line == d, DIGIT**d, scale)
    counts = jnp.sum(sums[channels:] * scale, axis=0, keepdims=True)
    below = jnp.maximum(counts, 1.0)
    divisor[...] = jnp.broadcast_to(below, divisor.shape)
    result = (sums[:channels] / below).astype(bf16)
    for h in range(pooled.shape[0]):
        pooled[h] = result


def fragment_kernel(
    table, mine, embed, message, update, cotangent, edge_from, target, out, partial, direct
):
    owners, channels, frag_dev = table.shape
    flat = table[...].reshape(owners * channels, frag_dev)
    owner, local = owner_and_local(edge_from[...], frag_dev)
    from_local = one_hot(local, frag_dev)
    source = pick(plain(flat, from_local), owner, owners).astype(bf16)
    pre_source = by_first(source, embed[...])
    sig_source = jax.nn.sigmoid(pre_source)
    own_source = (pre_source * sig_source).astype(bf16)
    pre_msg = plain(own_source, message[...])
    sig_msg = jax.nn.sigmoid(pre_msg)
    messages = (pre_msg * sig_msg).astype(bf16)
    to_target = one_hot(target[...], frag_dev)
    gathered = plain(to_target, messages).astype(bf16)
    pre_own = by_first(mine[...], embed[...])
    sig_own = jax.nn.sigmoid(pre_own)
    own = (pre_own * sig_own).astype(bf16)
    out[...] = (own.astype(f32) + plain(gathered, update[...])).astype(bf16)
    back_agg = by_last(cotangent[...], update[...]).astype(bf16)
    back_edge = by_first(to_target, back_agg)
    back_pre = (back_edge * slope_of(pre_msg, sig_msg)).astype(bf16)
    back_source = by_last(back_pre, message[...]) * slope_of(pre_source, sig_source)
    back_pooled = by_last(embed[...], back_source.astype(bf16))
    scattered = by_last(spread(back_pooled, owner, owners), from_local)
    partial[...] = scattered.reshape(partial.shape).astype(partial.dtype)
    near = cotangent[...].astype(f32) * slope_of(pre_own, sig_own)
    rough = near.astype(bf16)
    rest = (near - rough.astype(f32)).astype(bf16)
    direct[...] = by_last(embed[...], rough) + by_last(embed[...], rest)


def mean_kernel(parts, direct, divisor, mean):
    total = direct[...]
    for h in range(parts.shape[0]):
        total = total + parts[h].astype(f32)
    result = (total / divisor[:1]).astype(bf16)
    for h in range(mean.shape[0]):
        mean[h] = result


def hidden_kernel(
    table, fragment, lanes, sides, slopes_in, taps_in,
    hidden_out, conv_out, face_low, face_high, packed,
    slopes, back_hidden, back_conv, taps, grad, slopes_here, hidden_sent, conv_sent, taps_here
):
    owners, channels, frag_dev = table.shape
    rows, wide_height, _, depth = back_conv.shape
    height = wide_height - 2
    flat = table[...].reshape(owners * channels, frag_dev)
    fetch = row_copy(slopes_in, slopes, slopes_here)
    fetch_taps = row_copy(taps_in, taps, taps_here)
    send_hidden = row_copy(back_hidden, hidden_out, hidden_sent)
    send_conv = row_copy(back_conv, conv_out, conv_sent)
    start_rows(fetch, rows)
    start_rows(fetch_taps, rows + REACH - 1)
    empty = jnp.zeros((channels, depth), bf16)
    grad[...] = jnp.zeros_like(grad)
    wait_rows(fetch_taps, REACH - 1)

    def one_row(x, _):
        owner, local = owner_and_local(line_of(fragment[x]), frag_dev)
        owner = with_rims(owner.astype(f32), sides, x).astype(jnp.int32)
        local = with_rims(local.astype(f32), sides, rows + x).astype(jnp.int32)
        found = plain(flat, one_hot(local, frag_dev))
        hidden = pick(found, owner, owners)
        inner = hidden[:, depth : depth + height * depth]
        back_hidden[x] = (live_line(lanes, x, height) * inner).astype(bf16)
        send_hidden(x).start()
        fetch(x).wait()
        conv = (hidden * slopes[x].astype(f32)).astype(bf16)
        for y in range(wide_height):
            back_conv[x, y] = conv[:, y * depth : (y + 1) * depth]
        send_conv(x).start()
        fetch_taps(x + REACH - 1).wait()
        lines = []
        for b in range(REACH):
            parts = [empty] * b + [conv[:, depth : depth + height * depth]]
            lines.append(jnp.concatenate(parts + [empty] * (REACH - 1 - b), 1))
        stacked = jnp.concatenate(lines, 0)
        total = None
        for y in range(0, wide_height, 2):
            term = by_last(stacked[:, y * depth : (y + 2) * depth], columns(taps, x, y + 1, 2))
            total = term if total is None else total + term
        grad[...] += total
        return 0

    lax.fori_loop(0, rows, one_row, 0)
    face_low[...] = back_conv[0]
    face_high[...] = back_conv[rows - 1]
    packed[...] = jnp.zeros_like(packed)
    for place, part in packed_parts(grad.shape):
        high = part[0].stop - part[0].start
        width = part[1].stop - part[1].start
        packed[place[0] : place[0] + high, place[1] : place[1] + width] = grad[part]
    wait_rows(send_hidden, rows)
    wait_rows(send_conv, rows)


def packed_parts(shape):
    height, width = shape
    full = width // LANES * LANES
    rest = width - full
    parts = []
    for left in range(0, full, LANES):
        parts.append(((left // LANES * height, 0), (slice(0, height), slice(left, left + LANES))))
    if rest:
        folds = LANES // rest
        step = height // folds
        for k in range(folds):
            source = (slice(k * step, (k + 1) * step), slice(full, width))
            parts.append(((full // LANES * height, k * rest), source))
    return parts


def unpack(packed, shape):
    height, width = shape
    full = width // LANES * LANES
    rest = width - full
    blocks = [packed[left // LANES * height :][:height] for left in range(0, full, LANES)]
    if rest:
        folds = LANES // rest
        step = height // folds
        tail = packed[full // LANES * height :][:step]
        blocks.append(tail.reshape(step, folds, rest).swapaxes(0, 1).reshape(height, rest))
    return jnp.concatenate(blocks, 1)


def backward_kernel(
    back_conv, x_low, x_high, back_hidden, lanes, weight, grad_out,
    grad, taps, faces, sent, faces_here
):
    rows, wide_height, channels, depth = back_conv.shape
    height = wide_height - 2
    send = row_copy(grad, grad_out, sent)
    get_low = pltpu.make_async_copy(x_low, faces.at[0], faces_here.at[0])
    get_high = pltpu.make_async_copy(x_high, faces.at[1], faces_here.at[1])
    get_low.start()
    get_high.start()

    def fill(x, _):
        store_taps(taps, x + 1, 0, back_conv[x])
        return 0

    lax.fori_loop(0, rows, fill, 0)
    get_low.wait()
    get_high.wait()
    store_taps(taps, 0, 0, faces[0])
    store_taps(taps, rows + 1, 0, faces[1])

    def one_row(x, _):
        live = live_line(lanes, x, height)
        found = convolve_row(taps, weight[...], x, height)
        result = live * (back_hidden[x].astype(f32) + found)
        tiles = [result[:, y * depth : (y + 1) * depth][None] for y in range(height)]
        grad[x] = jnp.swapaxes(jnp.concatenate(tiles, 0), 0, 1)
        send(x).start()
        return 0

    lax.fori_loop(0, rows, one_row, 0)
    wait_rows(send, rows)


def cost(micros):
    return pl.CostEstimate(
        flops=micros * 10**9, bytes_accessed=micros * 3 * 10**6, transcendentals=0
    )


def call(kernel, shapes, *operands, scratch=(), micros=2, far_in=(), far_out=()):
    here, there = pl.BlockSpec(memory_space=pltpu.VMEM), pl.BlockSpec(memory_space=pl.ANY)
    return pl.pallas_call(
        kernel,
        in_specs=[there if i in far_in else here for i in range(len(operands))],
        out_specs=[there if i in far_out else here for i in range(len(shapes))],
        out_shape=[jax.ShapeDtypeStruct(shape, kind) for shape, kind in shapes],
        scratch_shapes=list(scratch),
        cost_estimate=cost(micros),
        compiler_params=pltpu.CompilerParams(vmem_limit_bytes=LIMIT),
    )(*operands)


def pass_on(low, high, axis):
    count = lax.axis_size(axis)
    up = [(i, i + 1) for i in range(count - 1)]
    down = [(i + 1, i) for i in range(count - 1)]
    return lax.ppermute(high, axis, up), lax.ppermute(low, axis, down)


def exchange(parts, axes):
    return lax.all_to_all(parts, axes, 0, 0, tiled=True)


def body(
    features,
    occupied,
    voxel_fragment,
    conv_weight,
    embed_weight,
    message_weight,
    update_weight,
    edge_source,
    edge_target,
    out_cotangent,
):
    rows, channels, height, depth = features.shape
    frag_dev, hid = out_cotangent.shape
    owners = lax.axis_size("beam")
    edge_count = edge_source.shape[0]
    plane = height * depth
    lanes = jnp.repeat(occupied, BLOCK, 2).astype(f32)
    gate = jnp.repeat(jnp.repeat(lanes, BLOCK, 0), BLOCK, 1).astype(bf16)

    split = conv_weight.reshape(channels, REACH, REACH, REACH, channels)
    stacked_shape = (REACH * channels, REACH * REACH * channels)
    stacked = split.transpose(2, 0, 1, 3, 4).reshape(stacked_shape)
    flipped = split[:, ::-1, ::-1, ::-1].transpose(2, 4, 1, 3, 0).reshape(stacked_shape)

    x_low, x_high = pass_on(
        features[0] * gate[0][None], features[-1] * gate[-1][None], "drift"
    )
    owner, local = owner_and_local(voxel_fragment, frag_dev)
    ends = []
    for edge, first in ((0, 0), (height - 1, height - RIM)):
        layers = slice(first, first + RIM)
        side = (features[:, :, layers] * gate[:, None, layers]).transpose(0, 2, 1, 3)
        outer = [x[:, layers].transpose(1, 0, 2) for x in (x_low, x_high)]
        notes = [owner[:, edge].astype(bf16), local[:, edge].astype(bf16), gate[:, edge]]
        notes.append(jnp.zeros((channels - 3 * rows, depth), bf16))
        flat = side.reshape(RIM * rows, channels, depth)
        ends.append(
            jnp.concatenate([outer[0], flat, outer[1], jnp.concatenate(notes, 0)[None]], 0)
        )
    y_low, y_high = pass_on(ends[0], ends[1], "beam")

    heads = -(-owners // 16) * 16
    line_shape = (rows, channels, plane)
    wide_shape = (rows, channels, plane + 2 * depth)
    conv_shape = (rows, height + 2, channels, depth)
    dma = lambda count: pltpu.SemaphoreType.DMA((count,))
    tapped = (rows + 2, height + 2, REACH * channels, depth)
    padded = (rows + 2, height + 2 * RIM, REACH * channels, depth)
    taps, slopes, partial, sides = call(
        forward_kernel,
        [
            (padded, bf16),
            (wide_shape, bf16),
            ((owners, channels + SPARE, frag_dev), bf16),
            ((2, channels, depth), f32),
        ],
        features, x_low, x_high, y_low, y_high, lanes, voxel_fragment, stacked, micros=12,
        scratch=[
            pltpu.VMEM(padded, bf16), pltpu.VMEM(wide_shape, bf16),
            pltpu.VMEM((owners * channels + heads, frag_dev), f32),
            pltpu.VMEM((2,) + y_low.shape, bf16), dma(rows + 2), dma(rows), dma(2),
        ],
        far_in=(3, 4), far_out=(0, 1),
    )
    spread_shape = (owners, channels, frag_dev)
    pooled, divisor = call(
        pool_kernel,
        [(spread_shape, bf16), ((8, frag_dev), f32)],
        exchange(partial, "beam"),
    )
    table = exchange(pooled, "beam")
    fragment_out, back_parts, direct = call(
        fragment_kernel,
        [((frag_dev, hid), bf16), (spread_shape, bf16), ((channels, frag_dev), f32)],
        table, pooled[0], embed_weight, message_weight, update_weight, out_cotangent,
        edge_source.reshape(1, edge_count),
        edge_target.reshape(1, edge_count),
    )
    (mean,) = call(
        mean_kernel, [(spread_shape, bf16)], exchange(back_parts, "beam"), direct, divisor
    )
    everyone = ("drift", "beam")
    devices = lax.axis_size(everyone)
    tile = SUBLANES * LANES
    share = -(-conv_weight.size // (devices * tile)) * SUBLANES
    back_hidden, back_conv, face_low, face_high, packed = call(
        hidden_kernel,
        [
            (line_shape, bf16), (conv_shape, bf16), (conv_shape[1:], bf16), (conv_shape[1:], bf16),
            ((devices * share, LANES), f32),
        ],
        exchange(mean, "beam"), voxel_fragment, lanes, sides, slopes, taps, micros=14,
        scratch=[
            pltpu.VMEM(wide_shape, bf16), pltpu.VMEM(line_shape, bf16),
            pltpu.VMEM(conv_shape, bf16), pltpu.VMEM(padded, bf16),
            pltpu.VMEM(stacked_shape, f32), dma(rows), dma(rows), dma(rows), dma(rows + 2),
        ],
        far_in=(4, 5), far_out=(0, 1),
    )
    gx_low, gx_high = pass_on(face_low, face_high, "drift")
    (grad_features,) = call(
        backward_kernel,
        [(features.shape, f32)],
        back_conv, gx_low, gx_high, back_hidden, lanes, flipped, micros=10,
        scratch=[
            pltpu.VMEM(features.shape, f32), pltpu.VMEM(tapped, bf16),
            pltpu.VMEM((2,) + conv_shape[1:], bf16), dma(rows), dma(2),
        ],
        far_in=(1, 2), far_out=(0,),
    )
    parts = exchange(packed, everyone).reshape(devices, share, LANES)
    full = exchange(jnp.broadcast_to(parts.sum(0)[None], parts.shape), everyone)
    grad_conv = (
        unpack(full.reshape(devices * share, LANES), stacked_shape)
        .reshape(REACH, channels, REACH, REACH, channels)
        .transpose(1, 2, 0, 3, 4)
        .reshape(conv_weight.shape)
    )
    return fragment_out, grad_features, grad_conv


def solution(mesh):
    return jax.shard_map(
        body,
        mesh=mesh,
        in_specs=(
            P("drift", None, "beam", None),
            P("drift", "beam", None),
            P("drift", "beam", None),
            P(),
            P(),
            P(),
            P(),
            P(("drift", "beam")),
            P(("drift", "beam")),
            P(("drift", "beam"), None),
        ),
        out_specs=(P(("drift", "beam"), None), P("drift", None, "beam", None), P()),
        check_vma=False,
    )
```

```python
import functools

import jax
import jax.numpy as jnp
from jax import lax
from jax.experimental import pallas as pl
from jax.experimental.pallas import tpu as pltpu
from jax.sharding import PartitionSpec as P

BLOCK = 8
REACH = 3
RIM = 2
SPARE = 16
LANES = 128
SUBLANES = 8
DIGIT = 128.0
LIMIT = 32 * 1024 * 1024
bf16 = jnp.bfloat16
f32 = jnp.float32


def contract(left, right, dims):
    return lax.dot_general(left, right, ((dims[0], dims[1]), ((), ())), preferred_element_type=f32)


def plain(left, right):
    return contract(left, right, ((1,), (0,)))


def by_last(left, right):
    return contract(left, right, ((1,), (1,)))


def by_first(left, right):
    return contract(left, right, ((0,), (0,)))


def slope_of(value, sig):
    return sig * (1.0 + value * (1.0 - sig))


def line_of(block):
    return jnp.concatenate([block[y : y + 1] for y in range(block.shape[0])], 1)


def live_line(lanes, row, height):
    bands = lanes[row // BLOCK]
    return jnp.concatenate([bands[y // BLOCK : y // BLOCK + 1] for y in range(height)], 1)


def with_rims(line, sides, place):
    return jnp.concatenate([sides[0, pl.ds(place, 1)], line, sides[1, pl.ds(place, 1)]], 1)


def owner_and_local(index, size):
    if size & (size - 1) == 0:
        return index >> (size.bit_length() - 1), index & (size - 1)
    return index // size, index % size


def one_hot(index, count):
    places = lax.broadcasted_iota(jnp.int32, (count, index.shape[-1]), 0)
    return jnp.where(places == index, 1.0, 0.0).astype(bf16)


def spread(values, owner, owners):
    parts = [jnp.where(owner == h, values, 0.0).astype(bf16) for h in range(owners)]
    return jnp.concatenate(parts, 0)


def pick(stacked, owner, owners):
    width = stacked.shape[0] // owners
    total = stacked[:width]
    for h in range(1, owners):
        total = jnp.where(owner == h, stacked[h * width : (h + 1) * width], total)
    return total


def store_taps(taps, row, first, tiles):
    count, channels, depth = tiles.shape
    flat = tiles.reshape(count * channels, depth)
    lane = lax.broadcasted_iota(jnp.int32, (1, depth), 1)
    after_first = jnp.where(lane == 0, 0.0, 1.0).astype(bf16)
    before_last = jnp.where(lane == depth - 1, 0.0, 1.0).astype(bf16)
    before = pltpu.roll(flat, 1, 1) * after_first
    after = pltpu.roll(flat, depth - 1, 1) * before_last
    for place, value in enumerate((before, flat, after)):
        taps[row, first : first + count, place * channels : (place + 1) * channels, :] = (
            value.reshape(count, channels, depth)
        )


def row_copy(source, target, arrived):
    return lambda x: pltpu.make_async_copy(source.at[x], target.at[x], arrived.at[x])


def wait_rows(copy, rows):
    def step(x, _):
        copy(x).wait()
        return 0

    lax.fori_loop(0, rows, step, 0)


def columns(taps, row, first, count):
    wide = []
    for y in range(first, first + count):
        wide.append(jnp.concatenate([taps[row + a, y] for a in range(REACH)], 0))
    return jnp.concatenate(wide, 1)


def convolve_row(taps, weight, row, height):
    depth = taps.shape[-1]
    channels = weight.shape[0] // REACH
    wide = height * depth
    found = jnp.concatenate(
        [plain(weight, columns(taps, row, y, 2)) for y in range(0, height + REACH - 1, 2)], 1
    )
    total = found[:channels, :wide]
    for b in range(1, REACH):
        part = found[b * channels : (b + 1) * channels, b * depth : b * depth + wide]
        total = total + part
    return total


def forward_kernel(
    feat, x_low, x_high, y_low, y_high, lanes, fragment, weight, _, taps, slopes, partial,
    sides, total, rims, rims_here
):
    rows, channels, height, depth = feat.shape
    owners, _, frag_dev = partial.shape

    def turned(block):
        return jnp.swapaxes(block.astype(f32), 0, 1)

    get_low = pltpu.make_async_copy(y_low, rims.at[0], rims_here.at[0])
    get_high = pltpu.make_async_copy(y_high, rims.at[1], rims_here.at[1])
    get_low.start()
    get_high.start()
    store_taps(taps, 0, RIM, turned(x_low[...]).astype(bf16))
    store_taps(taps, rows + 1, RIM, turned(x_high[...]).astype(bf16))

    def fill(x, _):
        tiles = turned(feat[x])
        live = live_line(lanes, x, height)
        gates = [live[:, y * depth : (y + 1) * depth] for y in range(height)]
        gates = jnp.concatenate([jnp.broadcast_to(g, (1, channels, depth)) for g in gates], 0)
        store_taps(taps, x + 1, RIM, (tiles * gates).astype(bf16))
        return 0

    lax.fori_loop(0, rows, fill, 0)
    get_low.wait()
    get_high.wait()

    def edges(x, _):
        store_taps(taps, x, 0, rims[0, pl.ds(RIM * x, RIM)])
        store_taps(taps, x, height + RIM, rims[1, pl.ds(RIM * x, RIM)])
        return 0

    lax.fori_loop(0, rows + 2, edges, 0)
    for side in range(2):
        sides[side] = rims[side, RIM * (rows + 2)].astype(f32)
    total[...] = jnp.zeros_like(total)

    def one_row(x, _):
        wide = convolve_row(taps, weight[...], x, height + 2)
        active = jnp.concatenate(
            [taps[x + 1, y + RIM, channels : 2 * channels, :] for y in range(height)], 1
        )
        live = live_line(lanes, x, height)
        owner, local = owner_and_local(line_of(fragment[x]), frag_dev)
        sig = jax.nn.sigmoid(wide)
        slopes[x] = (with_rims(live, sides, 2 * rows + x) * slope_of(wide, sig)).astype(bf16)
        inner = slice(depth, depth + height * depth)
        conv = wide[:, inner]
        hidden = live * (active.astype(f32) + conv * sig[:, inner])
        tallies = lax.broadcasted_iota(jnp.int32, (total.shape[0] - owners * channels, 1), 0)
        heads = jnp.where(tallies == owner, live, 0.0).astype(bf16)
        rising = jnp.concatenate([spread(hidden, owner, owners), heads], 0)
        total[...] += by_last(rising, one_hot(local, frag_dev))
        return 0

    lax.fori_loop(0, rows, one_row, 0)
    line = lax.broadcasted_iota(jnp.int32, (SPARE, frag_dev), 0)
    for h in range(owners):
        partial[h, :channels] = total[h * channels : (h + 1) * channels].astype(bf16)
        place = owners * channels + h
        rest = jnp.broadcast_to(total[place : place + 1], (SPARE, frag_dev))
        digits = jnp.zeros_like(rest)
        for d in range(SPARE):
            higher = jnp.floor(rest * (1.0 / DIGIT))
            digits = jnp.where(line == d, rest - higher * DIGIT, digits)
            rest = higher
            if DIGIT ** (d + 1) > rows * height * depth:
                break
        partial[h, channels:] = digits.astype(bf16)


def pool_kernel(parts, pooled, divisor):
    sums = parts[0].astype(f32)
    for h in range(1, parts.shape[0]):
        sums = sums + parts[h].astype(f32)
    channels = pooled.shape[1]
    line = lax.broadcasted_iota(jnp.int32, (SPARE, sums.shape[1]), 0)
    scale = jnp.zeros_like(sums[channels:])
    for d in range(4):
        scale = jnp.where(line == d, DIGIT**d, scale)
    counts = jnp.sum(sums[channels:] * scale, axis=0, keepdims=True)
    below = jnp.maximum(counts, 1.0)
    divisor[...] = jnp.broadcast_to(below, divisor.shape)
    result = (sums[:channels] / below).astype(bf16)
    for h in range(pooled.shape[0]):
        pooled[h] = result


def fragment_kernel(
    table, mine, embed, message, update, cotangent, edge_from, target, out, partial, direct
):
    owners, channels, frag_dev = table.shape
    flat = table[...].reshape(owners * channels, frag_dev)
    owner, local = owner_and_local(edge_from[...], frag_dev)
    from_local = one_hot(local, frag_dev)
    source = pick(plain(flat, from_local), owner, owners).astype(bf16)
    pre_source = by_first(source, embed[...])
    sig_source = jax.nn.sigmoid(pre_source)
    own_source = (pre_source * sig_source).astype(bf16)
    pre_msg = plain(own_source, message[...])
    sig_msg = jax.nn.sigmoid(pre_msg)
    messages = (pre_msg * sig_msg).astype(bf16)
    to_target = one_hot(target[...], frag_dev)
    gathered = plain(to_target, messages).astype(bf16)
    pre_own = by_first(mine[...], embed[...])
    sig_own = jax.nn.sigmoid(pre_own)
    own = (pre_own * sig_own).astype(bf16)
    out[...] = (own.astype(f32) + plain(gathered, update[...])).astype(bf16)
    back_agg = by_last(cotangent[...], update[...]).astype(bf16)
    back_edge = by_first(to_target, back_agg)
    back_pre = (back_edge * slope_of(pre_msg, sig_msg)).astype(bf16)
    back_source = by_last(back_pre, message[...]) * slope_of(pre_source, sig_source)
    back_pooled = by_last(embed[...], back_source.astype(bf16))
    scattered = by_last(spread(back_pooled, owner, owners), from_local)
    partial[...] = scattered.reshape(partial.shape).astype(partial.dtype)
    near = cotangent[...].astype(f32) * slope_of(pre_own, sig_own)
    rough = near.astype(bf16)
    rest = (near - rough.astype(f32)).astype(bf16)
    direct[...] = by_last(embed[...], rough) + by_last(embed[...], rest)


def mean_kernel(parts, direct, divisor, mean):
    total = direct[...]
    for h in range(parts.shape[0]):
        total = total + parts[h].astype(f32)
    result = (total / divisor[:1]).astype(bf16)
    for h in range(mean.shape[0]):
        mean[h] = result


def hidden_kernel(
    table, fragment, lanes, sides, slopes, taps,
    back_hidden, back_conv, face_low, face_high, packed, grad
):
    owners, channels, frag_dev = table.shape
    rows, wide_height, _, depth = back_conv.shape
    height = wide_height - 2
    flat = table[...].reshape(owners * channels, frag_dev)
    empty = jnp.zeros((channels, depth), bf16)
    grad[...] = jnp.zeros_like(grad)

    def one_row(x, _):
        owner, local = owner_and_local(line_of(fragment[x]), frag_dev)
        owner = with_rims(owner.astype(f32), sides, x).astype(jnp.int32)
        local = with_rims(local.astype(f32), sides, rows + x).astype(jnp.int32)
        pieces = []
        for y in range(0, wide_height, 2):
            here = slice(y * depth, (y + 2) * depth)
            found = plain(flat, one_hot(local[:, here], frag_dev))
            pieces.append(pick(found, owner[:, here], owners))
        hidden = jnp.concatenate(pieces, 1)
        inner = hidden[:, depth : depth + height * depth]
        back_hidden[x] = (live_line(lanes, x, height) * inner).astype(bf16)
        conv = (hidden * slopes[x].astype(f32)).astype(bf16)
        for y in range(wide_height):
            back_conv[x, y] = conv[:, y * depth : (y + 1) * depth]
        lines = []
        for b in range(REACH):
            parts = [empty] * b + [conv[:, depth : depth + height * depth]]
            lines.append(jnp.concatenate(parts + [empty] * (REACH - 1 - b), 1))
        stacked = jnp.concatenate(lines, 0)
        total = None
        for y in range(0, wide_height, 2):
            near = stacked[:, y * depth : (y + 2) * depth]
            term = by_last(columns(taps, x, y + 1, 2), near)
            total = term if total is None else total + term
        grad[...] += total
        return 0

    lax.fori_loop(0, rows, one_row, 0)
    face_low[...] = back_conv[0]
    face_high[...] = back_conv[rows - 1]
    packed[...] = jnp.zeros_like(packed)
    turned = grad[...].T
    for place, part in packed_parts(turned.shape):
        high = part[0].stop - part[0].start
        width = part[1].stop - part[1].start
        packed[place[0] : place[0] + high, place[1] : place[1] + width] = turned[part]


def packed_parts(shape):
    height, width = shape
    full = width // LANES * LANES
    rest = width - full
    parts = []
    for left in range(0, full, LANES):
        parts.append(((left // LANES * height, 0), (slice(0, height), slice(left, left + LANES))))
    if rest:
        folds = LANES // rest
        step = height // folds
        for k in range(folds):
            source = (slice(k * step, (k + 1) * step), slice(full, width))
            parts.append(((full // LANES * height, k * rest), source))
    return parts


def unpack(packed, shape):
    height, width = shape
    full = width // LANES * LANES
    rest = width - full
    blocks = [packed[left // LANES * height :][:height] for left in range(0, full, LANES)]
    if rest:
        folds = LANES // rest
        step = height // folds
        tail = packed[full // LANES * height :][:step]
        blocks.append(tail.reshape(step, folds, rest).swapaxes(0, 1).reshape(height, rest))
    return jnp.concatenate(blocks, 1)


def backward_kernel(
    back_conv, x_low, x_high, back_hidden, lanes, weight, grad_out,
    grad, taps, faces, sent, faces_here
):
    rows, wide_height, channels, depth = back_conv.shape
    height = wide_height - 2
    send = row_copy(grad, grad_out, sent)
    get_low = pltpu.make_async_copy(x_low, faces.at[0], faces_here.at[0])
    get_high = pltpu.make_async_copy(x_high, faces.at[1], faces_here.at[1])
    get_low.start()
    get_high.start()

    def fill(x, _):
        store_taps(taps, x + 1, 0, back_conv[x])
        return 0

    lax.fori_loop(0, rows, fill, 0)
    get_low.wait()
    get_high.wait()
    store_taps(taps, 0, 0, faces[0])
    store_taps(taps, rows + 1, 0, faces[1])

    def one_row(x, _):
        live = live_line(lanes, x, height)
        found = convolve_row(taps, weight[...], x, height)
        result = live * (back_hidden[x].astype(f32) + found)
        tiles = [result[:, y * depth : (y + 1) * depth][None] for y in range(height)]
        grad[x] = jnp.swapaxes(jnp.concatenate(tiles, 0), 0, 1)
        send(x).start()
        return 0

    lax.fori_loop(0, rows, one_row, 0)
    wait_rows(send, rows)


def cost(micros):
    return pl.CostEstimate(
        flops=micros * 10**9, bytes_accessed=micros * 3 * 10**6, transcendentals=0
    )


def call(kernel, shapes, *operands, scratch=(), micros=2, far_in=(), far_out=()):
    here, there = pl.BlockSpec(memory_space=pltpu.VMEM), pl.BlockSpec(memory_space=pl.ANY)
    return pl.pallas_call(
        kernel,
        in_specs=[there if i in far_in else here for i in range(len(operands))],
        out_specs=[there if i in far_out else here for i in range(len(shapes))],
        out_shape=[jax.ShapeDtypeStruct(shape, kind) for shape, kind in shapes],
        scratch_shapes=list(scratch),
        cost_estimate=cost(micros),
        compiler_params=pltpu.CompilerParams(vmem_limit_bytes=LIMIT),
    )(*operands)


def pass_on(low, high, axis):
    count = lax.axis_size(axis)
    up = [(i, i + 1) for i in range(count - 1)]
    down = [(i + 1, i) for i in range(count - 1)]
    return lax.ppermute(high, axis, up), lax.ppermute(low, axis, down)


def exchange(parts, axes):
    return lax.all_to_all(parts, axes, 0, 0, tiled=True)


def body(
    features,
    occupied,
    voxel_fragment,
    conv_weight,
    embed_weight,
    message_weight,
    update_weight,
    edge_source,
    edge_target,
    out_cotangent,
):
    rows, channels, height, depth = features.shape
    frag_dev, hid = out_cotangent.shape
    owners = lax.axis_size("beam")
    edge_count = edge_source.shape[0]
    plane = height * depth
    lanes = jnp.repeat(occupied, BLOCK, 2).astype(f32)
    gate = jnp.repeat(jnp.repeat(lanes, BLOCK, 0), BLOCK, 1).astype(bf16)

    split = conv_weight.reshape(channels, REACH, REACH, REACH, channels)
    stacked_shape = (REACH * channels, REACH * REACH * channels)
    stacked = split.transpose(2, 0, 1, 3, 4).reshape(stacked_shape)
    flipped = split[:, ::-1, ::-1, ::-1].transpose(2, 4, 1, 3, 0).reshape(stacked_shape)

    x_low, x_high = pass_on(
        features[0] * gate[0][None], features[-1] * gate[-1][None], "drift"
    )
    owner, local = owner_and_local(voxel_fragment, frag_dev)
    ends = []
    for edge, first in ((0, 0), (height - 1, height - RIM)):
        layers = slice(first, first + RIM)
        side = (features[:, :, layers] * gate[:, None, layers]).transpose(0, 2, 1, 3)
        outer = [x[:, layers].transpose(1, 0, 2) for x in (x_low, x_high)]
        notes = [owner[:, edge].astype(bf16), local[:, edge].astype(bf16), gate[:, edge]]
        notes.append(jnp.zeros((channels - 3 * rows, depth), bf16))
        flat = side.reshape(RIM * rows, channels, depth)
        ends.append(
            jnp.concatenate([outer[0], flat, outer[1], jnp.concatenate(notes, 0)[None]], 0)
        )
    y_low, y_high = pass_on(ends[0], ends[1], "beam")

    heads = -(-owners // 16) * 16
    line_shape = (rows, channels, plane)
    wide_shape = (rows, channels, plane + 2 * depth)
    conv_shape = (rows, height + 2, channels, depth)
    dma = lambda count: pltpu.SemaphoreType.DMA((count,))
    tapped = (rows + 2, height + 2, REACH * channels, depth)
    padded = (rows + 2, height + 2 * RIM, REACH * channels, depth)
    taps, slopes, partial, sides = call(
        forward_kernel,
        [
            (padded, bf16),
            (wide_shape, bf16),
            ((owners, channels + SPARE, frag_dev), bf16),
            ((2, channels, depth), f32),
        ],
        features, x_low, x_high, y_low, y_high, lanes, voxel_fragment, stacked, flipped, micros=12,
        scratch=[
            pltpu.VMEM((owners * channels + heads, frag_dev), f32),
            pltpu.VMEM((2,) + y_low.shape, bf16), dma(2),
        ],
        far_in=(3, 4, 8),
    )
    spread_shape = (owners, channels, frag_dev)
    pooled, divisor = call(
        pool_kernel,
        [(spread_shape, bf16), ((8, frag_dev), f32)],
        exchange(partial, "beam"),
    )
    table = exchange(pooled, "beam")
    fragment_out, back_parts, direct = call(
        fragment_kernel,
        [((frag_dev, hid), bf16), (spread_shape, bf16), ((channels, frag_dev), f32)],
        table, pooled[0], embed_weight, message_weight, update_weight, out_cotangent,
        edge_source.reshape(1, edge_count),
        edge_target.reshape(1, edge_count),
    )
    (mean,) = call(
        mean_kernel, [(spread_shape, bf16)], exchange(back_parts, "beam"), direct, divisor
    )
    everyone = ("drift", "beam")
    devices = lax.axis_size(everyone)
    tile = SUBLANES * LANES
    share = -(-conv_weight.size // (devices * tile)) * SUBLANES
    back_hidden, back_conv, face_low, face_high, packed = call(
        hidden_kernel,
        [
            (line_shape, bf16), (conv_shape, bf16), (conv_shape[1:], bf16), (conv_shape[1:], bf16),
            ((devices * share, LANES), f32),
        ],
        exchange(mean, "beam"), voxel_fragment, lanes, sides, slopes, taps, micros=14,
        scratch=[pltpu.VMEM(stacked_shape[::-1], f32)],
    )
    gx_low, gx_high = pass_on(face_low, face_high, "drift")
    (grad_features,) = call(
        backward_kernel,
        [(features.shape, f32)],
        back_conv, gx_low, gx_high, back_hidden, lanes, flipped, micros=10,
        scratch=[
            pltpu.VMEM(features.shape, f32), pltpu.VMEM(tapped, bf16),
            pltpu.VMEM((2,) + conv_shape[1:], bf16), dma(rows), dma(2),
        ],
        far_in=(1, 2), far_out=(0,),
    )
    parts = exchange(packed, everyone).reshape(devices, share, LANES)
    full = exchange(jnp.broadcast_to(parts.sum(0)[None], parts.shape), everyone)
    grad_conv = (
        unpack(full.reshape(devices * share, LANES), stacked_shape)
        .reshape(REACH, channels, REACH, REACH, channels)
        .transpose(1, 2, 0, 3, 4)
        .reshape(conv_weight.shape)
    )
    return fragment_out, grad_features, grad_conv


def solution(mesh):
    return jax.shard_map(
        body,
        mesh=mesh,
        in_specs=(
            P("drift", None, "beam", None),
            P("drift", "beam", None),
            P("drift", "beam", None),
            P(),
            P(),
            P(),
            P(),
            P(("drift", "beam")),
            P(("drift", "beam")),
            P(("drift", "beam"), None),
        ),
        out_specs=(P(("drift", "beam"), None), P("drift", None, "beam", None), P()),
        check_vma=False,
    )
```

```python
import functools

import jax
import jax.numpy as jnp
from jax import lax
from jax.experimental import pallas as pl
from jax.experimental.pallas import tpu as pltpu
from jax.sharding import PartitionSpec as P

BLOCK = 8
REACH = 3
RIM = 2
SPARE = 16
LANES = 128
SUBLANES = 8
DIGIT = 128.0
LIMIT = 24 * 1024 * 1024
bf16 = jnp.bfloat16
f32 = jnp.float32


def contract(left, right, dims):
    return lax.dot_general(left, right, ((dims[0], dims[1]), ((), ())), preferred_element_type=f32)


def plain(left, right):
    return contract(left, right, ((1,), (0,)))


def by_last(left, right):
    return contract(left, right, ((1,), (1,)))


def by_first(left, right):
    return contract(left, right, ((0,), (0,)))


def slope_of(value, sig):
    return sig * (1.0 + value * (1.0 - sig))


def line_of(block):
    return jnp.concatenate([block[y : y + 1] for y in range(block.shape[0])], 1)


def live_line(lanes, row, height):
    bands = lanes[row // BLOCK]
    return jnp.concatenate([bands[y // BLOCK : y // BLOCK + 1] for y in range(height)], 1)


def with_rims(line, sides, place):
    return jnp.concatenate([sides[0, pl.ds(place, 1)], line, sides[1, pl.ds(place, 1)]], 1)


def owner_and_local(index, size):
    if size & (size - 1) == 0:
        return index >> (size.bit_length() - 1), index & (size - 1)
    return index // size, index % size


def one_hot(index, count):
    places = lax.broadcasted_iota(jnp.int32, (count, index.shape[-1]), 0)
    return jnp.where(places == index, 1.0, 0.0).astype(bf16)


def spread(values, owner, owners):
    parts = [jnp.where(owner == h, values, 0.0).astype(bf16) for h in range(owners)]
    return jnp.concatenate(parts, 0)


def pick(stacked, owner, owners):
    width = stacked.shape[0] // owners
    total = stacked[:width]
    for h in range(1, owners):
        total = jnp.where(owner == h, stacked[h * width : (h + 1) * width], total)
    return total


def store_taps(taps, row, first, tiles):
    count, channels, depth = tiles.shape
    flat = tiles.reshape(count * channels, depth)
    lane = lax.broadcasted_iota(jnp.int32, (1, depth), 1)
    after_first = jnp.where(lane == 0, 0.0, 1.0).astype(bf16)
    before_last = jnp.where(lane == depth - 1, 0.0, 1.0).astype(bf16)
    before = pltpu.roll(flat, 1, 1) * after_first
    after = pltpu.roll(flat, depth - 1, 1) * before_last
    for place, value in enumerate((before, flat, after)):
        taps[row, first : first + count, place * channels : (place + 1) * channels, :] = (
            value.reshape(count, channels, depth)
        )


def row_copy(source, target, arrived):
    return lambda x: pltpu.make_async_copy(source.at[x], target.at[x], arrived.at[x])


def wait_rows(copy, rows):
    def step(x, _):
        copy(x).wait()
        return 0

    lax.fori_loop(0, rows, step, 0)


def tap(taps, row, y):
    for part in taps:
        if y < part.shape[1]:
            return part[row, y]
        y -= part.shape[1]


def columns(taps, row, first, count):
    wide = []
    for y in range(first, first + count):
        wide.append(jnp.concatenate([tap(taps, row + a, y) for a in range(REACH)], 0))
    return jnp.concatenate(wide, 1)


def convolve_row(taps, weight, row, height):
    depth = taps[0].shape[-1]
    channels = weight.shape[0] // REACH
    wide = height * depth
    found = jnp.concatenate(
        [plain(weight, columns(taps, row, y, 2)) for y in range(0, height + REACH - 1, 2)], 1
    )
    total = found[:channels, :wide]
    for b in range(1, REACH):
        part = found[b * channels : (b + 1) * channels, b * depth : b * depth + wide]
        total = total + part
    return total


def inner_kernel(feat, x_low, x_high, lanes, core):
    rows, channels, height, depth = feat.shape

    def turned(block):
        return jnp.swapaxes(block.astype(f32), 0, 1)

    store_taps(core, 0, 0, turned(x_low[...]).astype(bf16))
    store_taps(core, rows + 1, 0, turned(x_high[...]).astype(bf16))

    def fill(x, _):
        tiles = turned(feat[x])
        live = live_line(lanes, x, height)
        gates = [live[:, y * depth : (y + 1) * depth] for y in range(height)]
        gates = jnp.concatenate([jnp.broadcast_to(g, (1, channels, depth)) for g in gates], 0)
        store_taps(core, x + 1, 0, (tiles * gates).astype(bf16))
        return 0

    lax.fori_loop(0, rows, fill, 0)


def forward_kernel(
    core, y_low, y_high, lanes, fragment, weight, low, high, slopes, partial,
    sides, total, rims, rims_here
):
    owners, _, frag_dev = partial.shape
    height = core.shape[1]
    rows, channels, wide = slopes.shape
    depth = wide // (height + 2)
    taps = (low, core, high)
    get_low = pltpu.make_async_copy(y_low, rims.at[0], rims_here.at[0])
    get_high = pltpu.make_async_copy(y_high, rims.at[1], rims_here.at[1])
    get_low.start()
    get_high.start()
    get_low.wait()
    get_high.wait()

    def edges(x, _):
        store_taps(low, x, 0, rims[0, pl.ds(RIM * x, RIM)])
        store_taps(high, x, 0, rims[1, pl.ds(RIM * x, RIM)])
        return 0

    lax.fori_loop(0, rows + 2, edges, 0)
    for side in range(2):
        sides[side] = rims[side, RIM * (rows + 2)].astype(f32)
    total[...] = jnp.zeros_like(total)

    def one_row(x, _):
        wide = convolve_row(taps, weight[...], x, height + 2)
        active = jnp.concatenate(
            [core[x + 1, y, channels : 2 * channels, :] for y in range(height)], 1
        )
        live = live_line(lanes, x, height)
        owner, local = owner_and_local(line_of(fragment[x]), frag_dev)
        sig = jax.nn.sigmoid(wide)
        slopes[x] = (with_rims(live, sides, 2 * rows + x) * slope_of(wide, sig)).astype(bf16)
        inner = slice(depth, depth + height * depth)
        conv = wide[:, inner]
        hidden = live * (active.astype(f32) + conv * sig[:, inner])
        tallies = lax.broadcasted_iota(jnp.int32, (total.shape[0] - owners * channels, 1), 0)
        heads = jnp.where(tallies == owner, live, 0.0).astype(bf16)
        rising = jnp.concatenate([spread(hidden, owner, owners), heads], 0)
        total[...] += by_last(rising, one_hot(local, frag_dev))
        return 0

    lax.fori_loop(0, rows, one_row, 0)
    line = lax.broadcasted_iota(jnp.int32, (SPARE, frag_dev), 0)
    for h in range(owners):
        partial[h, :channels] = total[h * channels : (h + 1) * channels].astype(bf16)
        place = owners * channels + h
        rest = jnp.broadcast_to(total[place : place + 1], (SPARE, frag_dev))
        digits = jnp.zeros_like(rest)
        for d in range(SPARE):
            higher = jnp.floor(rest * (1.0 / DIGIT))
            digits = jnp.where(line == d, rest - higher * DIGIT, digits)
            rest = higher
            if DIGIT ** (d + 1) > rows * height * depth:
                break
        partial[h, channels:] = digits.astype(bf16)


def pool_kernel(parts, pooled, divisor):
    sums = parts[0].astype(f32)
    for h in range(1, parts.shape[0]):
        sums = sums + parts[h].astype(f32)
    channels = pooled.shape[1]
    line = lax.broadcasted_iota(jnp.int32, (SPARE, sums.shape[1]), 0)
    scale = jnp.zeros_like(sums[channels:])
    for d in range(4):
        scale = jnp.where(line == d, DIGIT**d, scale)
    counts = jnp.sum(sums[channels:] * scale, axis=0, keepdims=True)
    below = jnp.maximum(counts, 1.0)
    divisor[...] = jnp.broadcast_to(below, divisor.shape)
    result = (sums[:channels] / below).astype(bf16)
    for h in range(pooled.shape[0]):
        pooled[h] = result


def fragment_kernel(
    table, mine, embed, message, update, cotangent, edge_from, target, _, out, partial, direct
):
    owners, channels, frag_dev = table.shape
    flat = table[...].reshape(owners * channels, frag_dev)
    owner, local = owner_and_local(edge_from[...], frag_dev)
    from_local = one_hot(local, frag_dev)
    source = pick(plain(flat, from_local), owner, owners).astype(bf16)
    pre_source = by_first(source, embed[...])
    sig_source = jax.nn.sigmoid(pre_source)
    own_source = (pre_source * sig_source).astype(bf16)
    pre_msg = plain(own_source, message[...])
    sig_msg = jax.nn.sigmoid(pre_msg)
    messages = (pre_msg * sig_msg).astype(bf16)
    to_target = one_hot(target[...], frag_dev)
    gathered = plain(to_target, messages).astype(bf16)
    pre_own = by_first(mine[...], embed[...])
    sig_own = jax.nn.sigmoid(pre_own)
    own = (pre_own * sig_own).astype(bf16)
    out[...] = (own.astype(f32) + plain(gathered, update[...])).astype(bf16)
    back_agg = by_last(cotangent[...], update[...]).astype(bf16)
    back_edge = by_first(to_target, back_agg)
    back_pre = (back_edge * slope_of(pre_msg, sig_msg)).astype(bf16)
    back_source = by_last(back_pre, message[...]) * slope_of(pre_source, sig_source)
    back_pooled = by_last(embed[...], back_source.astype(bf16))
    scattered = by_last(spread(back_pooled, owner, owners), from_local)
    partial[...] = scattered.reshape(partial.shape).astype(partial.dtype)
    near = cotangent[...].astype(f32) * slope_of(pre_own, sig_own)
    rough = near.astype(bf16)
    rest = (near - rough.astype(f32)).astype(bf16)
    direct[...] = by_last(embed[...], rough) + by_last(embed[...], rest)


def mean_kernel(parts, direct, divisor, mean):
    total = direct[...]
    for h in range(parts.shape[0]):
        total = total + parts[h].astype(f32)
    result = (total / divisor[:1]).astype(bf16)
    for h in range(mean.shape[0]):
        mean[h] = result


def hidden_kernel(
    table, fragment, lanes, sides, slopes, low, core, high,
    back_hidden, back_conv, face_low, face_high, packed, grad
):
    owners, channels, frag_dev = table.shape
    rows, wide_height, _, depth = back_conv.shape
    height = wide_height - 2
    taps = (low, core, high)
    flat = table[...].reshape(owners * channels, frag_dev)
    empty = jnp.zeros((channels, depth), bf16)
    grad[...] = jnp.zeros_like(grad)

    def one_row(x, _):
        owner, local = owner_and_local(line_of(fragment[x]), frag_dev)
        owner = with_rims(owner.astype(f32), sides, x).astype(jnp.int32)
        local = with_rims(local.astype(f32), sides, rows + x).astype(jnp.int32)
        pieces = []
        for y in range(0, wide_height, 2):
            here = slice(y * depth, (y + 2) * depth)
            found = plain(flat, one_hot(local[:, here], frag_dev))
            pieces.append(pick(found, owner[:, here], owners))
        hidden = jnp.concatenate(pieces, 1)
        inner = hidden[:, depth : depth + height * depth]
        back_hidden[x] = (live_line(lanes, x, height) * inner).astype(bf16)
        conv = (hidden * slopes[x].astype(f32)).astype(bf16)
        for y in range(wide_height):
            back_conv[x, y] = conv[:, y * depth : (y + 1) * depth]
        lines = []
        for b in range(REACH):
            parts = [empty] * b + [conv[:, depth : depth + height * depth]]
            lines.append(jnp.concatenate(parts + [empty] * (REACH - 1 - b), 1))
        stacked = jnp.concatenate(lines, 0)
        total = None
        for y in range(0, wide_height, 2):
            near = stacked[:, y * depth : (y + 2) * depth]
            term = by_last(columns(taps, x, y + 1, 2), near)
            total = term if total is None else total + term
        grad[...] += total
        return 0

    lax.fori_loop(0, rows, one_row, 0)
    face_low[...] = back_conv[0]
    face_high[...] = back_conv[rows - 1]
    packed[...] = jnp.zeros_like(packed)
    turned = grad[...].T
    for place, part in packed_parts(turned.shape):
        high = part[0].stop - part[0].start
        width = part[1].stop - part[1].start
        packed[place[0] : place[0] + high, place[1] : place[1] + width] = turned[part]


def packed_parts(shape):
    height, width = shape
    full = width // LANES * LANES
    rest = width - full
    parts = []
    for left in range(0, full, LANES):
        parts.append(((left // LANES * height, 0), (slice(0, height), slice(left, left + LANES))))
    if rest:
        folds = LANES // rest
        step = height // folds
        for k in range(folds):
            source = (slice(k * step, (k + 1) * step), slice(full, width))
            parts.append(((full // LANES * height, k * rest), source))
    return parts


def unpack(packed, shape):
    height, width = shape
    full = width // LANES * LANES
    rest = width - full
    blocks = [packed[left // LANES * height :][:height] for left in range(0, full, LANES)]
    if rest:
        folds = LANES // rest
        step = height // folds
        tail = packed[full // LANES * height :][:step]
        blocks.append(tail.reshape(step, folds, rest).swapaxes(0, 1).reshape(height, rest))
    return jnp.concatenate(blocks, 1)


def backward_kernel(
    back_conv, x_low, x_high, back_hidden, lanes, weight, grad_out,
    grad, taps, faces, sent, faces_here
):
    rows, wide_height, channels, depth = back_conv.shape
    height = wide_height - 2
    send = row_copy(grad, grad_out, sent)
    get_low = pltpu.make_async_copy(x_low, faces.at[0], faces_here.at[0])
    get_high = pltpu.make_async_copy(x_high, faces.at[1], faces_here.at[1])
    get_low.start()
    get_high.start()

    def fill(x, _):
        store_taps(taps, x + 1, 0, back_conv[x])
        return 0

    lax.fori_loop(0, rows, fill, 0)
    get_low.wait()
    get_high.wait()
    store_taps(taps, 0, 0, faces[0])
    store_taps(taps, rows + 1, 0, faces[1])

    def one_row(x, _):
        live = live_line(lanes, x, height)
        found = convolve_row((taps,), weight[...], x, height)
        result = live * (back_hidden[x].astype(f32) + found)
        tiles = [result[:, y * depth : (y + 1) * depth][None] for y in range(height)]
        grad[x] = jnp.swapaxes(jnp.concatenate(tiles, 0), 0, 1)
        send(x).start()
        return 0

    lax.fori_loop(0, rows, one_row, 0)
    wait_rows(send, rows)


def cost(micros):
    return pl.CostEstimate(
        flops=micros * 10**9, bytes_accessed=micros * 3 * 10**6, transcendentals=0
    )


def call(kernel, shapes, *operands, scratch=(), micros=2, far_in=(), far_out=()):
    here, there = pl.BlockSpec(memory_space=pltpu.VMEM), pl.BlockSpec(memory_space=pl.ANY)
    return pl.pallas_call(
        kernel,
        in_specs=[there if i in far_in else here for i in range(len(operands))],
        out_specs=[there if i in far_out else here for i in range(len(shapes))],
        out_shape=[jax.ShapeDtypeStruct(shape, kind) for shape, kind in shapes],
        scratch_shapes=list(scratch),
        cost_estimate=cost(micros),
        compiler_params=pltpu.CompilerParams(vmem_limit_bytes=LIMIT),
    )(*operands)


def pass_on(low, high, axis):
    count = lax.axis_size(axis)
    up = [(i, i + 1) for i in range(count - 1)]
    down = [(i + 1, i) for i in range(count - 1)]
    return lax.ppermute(high, axis, up), lax.ppermute(low, axis, down)


def exchange(parts, axes):
    return lax.all_to_all(parts, axes, 0, 0, tiled=True)


def body(
    features,
    occupied,
    voxel_fragment,
    conv_weight,
    embed_weight,
    message_weight,
    update_weight,
    edge_source,
    edge_target,
    out_cotangent,
):
    rows, channels, height, depth = features.shape
    frag_dev, hid = out_cotangent.shape
    owners = lax.axis_size("beam")
    edge_count = edge_source.shape[0]
    plane = height * depth
    lanes = jnp.repeat(occupied, BLOCK, 2).astype(f32)
    gate = jnp.repeat(jnp.repeat(lanes, BLOCK, 0), BLOCK, 1).astype(bf16)

    split = conv_weight.reshape(channels, REACH, REACH, REACH, channels)
    stacked_shape = (REACH * channels, REACH * REACH * channels)
    stacked = split.transpose(2, 0, 1, 3, 4).reshape(stacked_shape)
    flipped = split[:, ::-1, ::-1, ::-1].transpose(2, 4, 1, 3, 0).reshape(stacked_shape)

    x_low, x_high = pass_on(
        features[0] * gate[0][None], features[-1] * gate[-1][None], "drift"
    )
    owner, local = owner_and_local(voxel_fragment, frag_dev)
    ends = []
    for edge, first in ((0, 0), (height - 1, height - RIM)):
        layers = slice(first, first + RIM)
        side = (features[:, :, layers] * gate[:, None, layers]).transpose(0, 2, 1, 3)
        outer = [x[:, layers].transpose(1, 0, 2) for x in (x_low, x_high)]
        notes = [owner[:, edge].astype(bf16), local[:, edge].astype(bf16), gate[:, edge]]
        notes.append(jnp.zeros((channels - 3 * rows, depth), bf16))
        flat = side.reshape(RIM * rows, channels, depth)
        ends.append(
            jnp.concatenate([outer[0], flat, outer[1], jnp.concatenate(notes, 0)[None]], 0)
        )
    y_low, y_high = pass_on(ends[0], ends[1], "beam")

    heads = -(-owners // 16) * 16
    line_shape = (rows, channels, plane)
    wide_shape = (rows, channels, plane + 2 * depth)
    conv_shape = (rows, height + 2, channels, depth)
    dma = lambda count: pltpu.SemaphoreType.DMA((count,))
    tapped = (rows + 2, height + 2, REACH * channels, depth)
    inner_shape = (rows + 2, height, REACH * channels, depth)
    rim_shape = (rows + 2, RIM, REACH * channels, depth)
    (core,) = call(
        inner_kernel, [(inner_shape, bf16)], features, x_low, x_high, lanes, micros=3
    )
    low, high, slopes, partial, sides = call(
        forward_kernel,
        [
            (rim_shape, bf16),
            (rim_shape, bf16),
            (wide_shape, bf16),
            ((owners, channels + SPARE, frag_dev), bf16),
            ((2, channels, depth), f32),
        ],
        core, y_low, y_high, lanes, voxel_fragment, stacked, micros=9,
        scratch=[
            pltpu.VMEM((owners * channels + heads, frag_dev), f32),
            pltpu.VMEM((2,) + y_low.shape, bf16), dma(2),
        ],
        far_in=(1, 2),
    )
    spread_shape = (owners, channels, frag_dev)
    pooled, divisor = call(
        pool_kernel,
        [(spread_shape, bf16), ((8, frag_dev), f32)],
        exchange(partial, "beam"),
    )
    table = exchange(pooled, "beam")
    fragment_out, back_parts, direct = call(
        fragment_kernel,
        [((frag_dev, hid), bf16), (spread_shape, bf16), ((channels, frag_dev), f32)],
        table, pooled[0], embed_weight, message_weight, update_weight, out_cotangent,
        edge_source.reshape(1, edge_count),
        edge_target.reshape(1, edge_count), flipped, far_in=(8,),
    )
    (mean,) = call(
        mean_kernel, [(spread_shape, bf16)], exchange(back_parts, "beam"), direct, divisor
    )
    everyone = ("drift", "beam")
    devices = lax.axis_size(everyone)
    tile = SUBLANES * LANES
    share = -(-conv_weight.size // (devices * tile)) * SUBLANES
    back_hidden, back_conv, face_low, face_high, packed = call(
        hidden_kernel,
        [
            (line_shape, bf16), (conv_shape, bf16), (conv_shape[1:], bf16), (conv_shape[1:], bf16),
            ((devices * share, LANES), f32),
        ],
        exchange(mean, "beam"), voxel_fragment, lanes, sides, slopes, low, core, high, micros=9,
        scratch=[pltpu.VMEM(stacked_shape[::-1], f32)],
    )
    gx_low, gx_high = pass_on(face_low, face_high, "drift")
    (grad_features,) = call(
        backward_kernel,
        [(features.shape, f32)],
        back_conv, gx_low, gx_high, back_hidden, lanes, flipped, micros=10,
        scratch=[
            pltpu.VMEM(features.shape, f32), pltpu.VMEM(tapped, bf16),
            pltpu.VMEM((2,) + conv_shape[1:], bf16), dma(rows), dma(2),
        ],
        far_in=(1, 2), far_out=(0,),
    )
    parts = exchange(packed, everyone).reshape(devices, share, LANES)
    full = exchange(jnp.broadcast_to(parts.sum(0)[None], parts.shape), everyone)
    grad_conv = (
        unpack(full.reshape(devices * share, LANES), stacked_shape)
        .reshape(REACH, channels, REACH, REACH, channels)
        .transpose(1, 2, 0, 3, 4)
        .reshape(conv_weight.shape)
    )
    return fragment_out, grad_features, grad_conv


def solution(mesh):
    return jax.shard_map(
        body,
        mesh=mesh,
        in_specs=(
            P("drift", None, "beam", None),
            P("drift", "beam", None),
            P("drift", "beam", None),
            P(),
            P(),
            P(),
            P(),
            P(("drift", "beam")),
            P(("drift", "beam")),
            P(("drift", "beam"), None),
        ),
        out_specs=(P(("drift", "beam"), None), P("drift", None, "beam", None), P()),
        check_vma=False,
    )
```

```python
import functools

import jax
import jax.numpy as jnp
from jax import lax
from jax.experimental import pallas as pl
from jax.experimental.pallas import tpu as pltpu
from jax.sharding import PartitionSpec as P

BLOCK = 8
REACH = 3
RIM = 2
SPARE = 16
LANES = 128
SUBLANES = 8
DIGIT = 128.0
LIMIT = 24 * 1024 * 1024
bf16 = jnp.bfloat16
f32 = jnp.float32


def contract(left, right, dims):
    return lax.dot_general(left, right, ((dims[0], dims[1]), ((), ())), preferred_element_type=f32)


def plain(left, right):
    return contract(left, right, ((1,), (0,)))


def by_last(left, right):
    return contract(left, right, ((1,), (1,)))


def by_first(left, right):
    return contract(left, right, ((0,), (0,)))


def slope_of(value, sig):
    return sig * (1.0 + value * (1.0 - sig))


def line_of(block):
    return jnp.concatenate([block[y : y + 1] for y in range(block.shape[0])], 1)


def live_line(lanes, row, height):
    bands = lanes[row // BLOCK]
    return jnp.concatenate([bands[y // BLOCK : y // BLOCK + 1] for y in range(height)], 1)


def with_rims(line, sides, place):
    return jnp.concatenate([sides[0, pl.ds(place, 1)], line, sides[1, pl.ds(place, 1)]], 1)


def owner_and_local(index, size):
    if size & (size - 1) == 0:
        return index >> (size.bit_length() - 1), index & (size - 1)
    return index // size, index % size


def one_hot(index, count):
    places = lax.broadcasted_iota(jnp.int32, (count, index.shape[-1]), 0)
    return jnp.where(places == index, 1.0, 0.0).astype(bf16)


def spread(values, owner, owners):
    parts = [jnp.where(owner == h, values, 0.0).astype(bf16) for h in range(owners)]
    return jnp.concatenate(parts, 0)


def pick(stacked, owner, owners):
    width = stacked.shape[0] // owners
    total = stacked[:width]
    for h in range(1, owners):
        total = jnp.where(owner == h, stacked[h * width : (h + 1) * width], total)
    return total


def store_taps(taps, row, first, tiles):
    count, channels, depth = tiles.shape
    flat = tiles.reshape(count * channels, depth)
    lane = lax.broadcasted_iota(jnp.int32, (1, depth), 1)
    after_first = jnp.where(lane == 0, 0.0, 1.0).astype(bf16)
    before_last = jnp.where(lane == depth - 1, 0.0, 1.0).astype(bf16)
    before = pltpu.roll(flat, 1, 1) * after_first
    after = pltpu.roll(flat, depth - 1, 1) * before_last
    for place, value in enumerate((before, flat, after)):
        taps[row, first : first + count, place * channels : (place + 1) * channels, :] = (
            value.reshape(count, channels, depth)
        )


def row_copy(source, target, arrived):
    return lambda x: pltpu.make_async_copy(source.at[x], target.at[x], arrived.at[x])


def wait_rows(copy, rows):
    def step(x, _):
        copy(x).wait()
        return 0

    lax.fori_loop(0, rows, step, 0)


def tap(taps, row, y):
    for part in taps:
        if y < part.shape[1]:
            return part[row, y]
        y -= part.shape[1]


def columns(taps, row, first, count):
    wide = []
    for y in range(first, first + count):
        wide.append(jnp.concatenate([tap(taps, row + a, y) for a in range(REACH)], 0))
    return jnp.concatenate(wide, 1)


def convolve_row(taps, weight, row, height):
    depth = taps[0].shape[-1]
    channels = weight.shape[0] // REACH
    wide = height * depth
    found = jnp.concatenate(
        [plain(weight, columns(taps, row, y, 2)) for y in range(0, height + REACH - 1, 2)], 1
    )
    total = found[:channels, :wide]
    for b in range(1, REACH):
        part = found[b * channels : (b + 1) * channels, b * depth : b * depth + wide]
        total = total + part
    return total


def inner_kernel(feat, x_low, x_high, lanes, core):
    rows, channels, height, depth = feat.shape

    def turned(block):
        return jnp.swapaxes(block.astype(f32), 0, 1)

    store_taps(core, 0, 0, turned(x_low[...]).astype(bf16))
    store_taps(core, rows + 1, 0, turned(x_high[...]).astype(bf16))

    def fill(x, _):
        tiles = turned(feat[x])
        live = live_line(lanes, x, height)
        gates = [live[:, y * depth : (y + 1) * depth] for y in range(height)]
        gates = jnp.concatenate([jnp.broadcast_to(g, (1, channels, depth)) for g in gates], 0)
        store_taps(core, x + 1, 0, (tiles * gates).astype(bf16))
        return 0

    lax.fori_loop(0, rows, fill, 0)


def forward_kernel(
    core, y_low, y_high, lanes, fragment, weight, low, high, slopes, partial,
    sides, total, rims, rims_here
):
    owners, _, frag_dev = partial.shape
    height = core.shape[1]
    rows, channels, wide = slopes.shape
    depth = wide // (height + 2)
    taps = (low, core, high)
    get_low = pltpu.make_async_copy(y_low, rims.at[0], rims_here.at[0])
    get_high = pltpu.make_async_copy(y_high, rims.at[1], rims_here.at[1])
    get_low.start()
    get_high.start()
    get_low.wait()
    get_high.wait()

    def edges(x, _):
        store_taps(low, x, 0, rims[0, pl.ds(RIM * x, RIM)])
        store_taps(high, x, 0, rims[1, pl.ds(RIM * x, RIM)])
        return 0

    lax.fori_loop(0, rows + 2, edges, 0)
    for side in range(2):
        sides[side] = rims[side, RIM * (rows + 2)].astype(f32)
    total[...] = jnp.zeros_like(total)

    def one_row(x, _):
        wide = convolve_row(taps, weight[...], x, height + 2)
        active = jnp.concatenate(
            [core[x + 1, y, channels : 2 * channels, :] for y in range(height)], 1
        )
        live = live_line(lanes, x, height)
        owner, local = owner_and_local(line_of(fragment[x]), frag_dev)
        sig = jax.nn.sigmoid(wide)
        slopes[x] = (with_rims(live, sides, 2 * rows + x) * slope_of(wide, sig)).astype(bf16)
        inner = slice(depth, depth + height * depth)
        conv = wide[:, inner]
        hidden = live * (active.astype(f32) + conv * sig[:, inner])
        tallies = lax.broadcasted_iota(jnp.int32, (total.shape[0] - owners * channels, 1), 0)
        heads = jnp.where(tallies == owner, live, 0.0).astype(bf16)
        rising = jnp.concatenate([spread(hidden, owner, owners), heads], 0)
        total[...] += by_last(rising, one_hot(local, frag_dev))
        return 0

    lax.fori_loop(0, rows, one_row, 0)
    line = lax.broadcasted_iota(jnp.int32, (SPARE, frag_dev), 0)
    for h in range(owners):
        partial[h, :channels] = total[h * channels : (h + 1) * channels].astype(bf16)
        place = owners * channels + h
        rest = jnp.broadcast_to(total[place : place + 1], (SPARE, frag_dev))
        digits = jnp.zeros_like(rest)
        for d in range(SPARE):
            higher = jnp.floor(rest * (1.0 / DIGIT))
            digits = jnp.where(line == d, rest - higher * DIGIT, digits)
            rest = higher
            if DIGIT ** (d + 1) > rows * height * depth:
                break
        partial[h, channels:] = digits.astype(bf16)


def pool_kernel(parts, pooled, divisor):
    sums = parts[0].astype(f32)
    for h in range(1, parts.shape[0]):
        sums = sums + parts[h].astype(f32)
    channels = pooled.shape[1]
    line = lax.broadcasted_iota(jnp.int32, (SPARE, sums.shape[1]), 0)
    scale = jnp.zeros_like(sums[channels:])
    for d in range(4):
        scale = jnp.where(line == d, DIGIT**d, scale)
    counts = jnp.sum(sums[channels:] * scale, axis=0, keepdims=True)
    below = jnp.maximum(counts, 1.0)
    divisor[...] = jnp.broadcast_to(below, divisor.shape)
    result = (sums[:channels] / below).astype(bf16)
    for h in range(pooled.shape[0]):
        pooled[h] = result


def fragment_kernel(
    table, mine, embed, message, update, cotangent, edge_from, target, _, out, partial, direct
):
    owners, channels, frag_dev = table.shape
    flat = table[...].reshape(owners * channels, frag_dev)
    owner, local = owner_and_local(edge_from[...], frag_dev)
    from_local = one_hot(local, frag_dev)
    source = pick(plain(flat, from_local), owner, owners).astype(bf16)
    pre_source = by_first(source, embed[...])
    sig_source = jax.nn.sigmoid(pre_source)
    own_source = (pre_source * sig_source).astype(bf16)
    pre_msg = plain(own_source, message[...])
    sig_msg = jax.nn.sigmoid(pre_msg)
    messages = (pre_msg * sig_msg).astype(bf16)
    to_target = one_hot(target[...], frag_dev)
    gathered = plain(to_target, messages).astype(bf16)
    pre_own = by_first(mine[...], embed[...])
    sig_own = jax.nn.sigmoid(pre_own)
    own = (pre_own * sig_own).astype(bf16)
    out[...] = (own.astype(f32) + plain(gathered, update[...])).astype(bf16)
    back_agg = by_last(cotangent[...], update[...]).astype(bf16)
    back_edge = by_first(to_target, back_agg)
    back_pre = (back_edge * slope_of(pre_msg, sig_msg)).astype(bf16)
    back_source = by_last(back_pre, message[...]) * slope_of(pre_source, sig_source)
    back_pooled = by_last(embed[...], back_source.astype(bf16))
    scattered = by_last(spread(back_pooled, owner, owners), from_local)
    partial[...] = scattered.reshape(partial.shape).astype(partial.dtype)
    near = cotangent[...].astype(f32) * slope_of(pre_own, sig_own)
    rough = near.astype(bf16)
    rest = (near - rough.astype(f32)).astype(bf16)
    direct[...] = by_last(embed[...], rough) + by_last(embed[...], rest)


def mean_kernel(parts, direct, divisor, mean):
    total = direct[...]
    for h in range(parts.shape[0]):
        total = total + parts[h].astype(f32)
    result = (total / divisor[:1]).astype(bf16)
    for h in range(mean.shape[0]):
        mean[h] = result


def hidden_kernel(
    table, fragment, lanes, sides, slopes, low, core, high,
    hidden_out, back_conv, face_low, face_high, packed, grad, back_hidden, hidden_sent
):
    owners, channels, frag_dev = table.shape
    rows, wide_height, _, depth = back_conv.shape
    height = wide_height - 2
    taps = (low, core, high)
    send = row_copy(back_hidden, hidden_out, hidden_sent)
    flat = table[...].reshape(owners * channels, frag_dev)
    empty = jnp.zeros((channels, depth), bf16)
    grad[...] = jnp.zeros_like(grad)

    def one_row(x, _):
        owner, local = owner_and_local(line_of(fragment[x]), frag_dev)
        owner = with_rims(owner.astype(f32), sides, x).astype(jnp.int32)
        local = with_rims(local.astype(f32), sides, rows + x).astype(jnp.int32)
        pieces = []
        for y in range(0, wide_height, 2):
            here = slice(y * depth, (y + 2) * depth)
            found = plain(flat, one_hot(local[:, here], frag_dev))
            pieces.append(pick(found, owner[:, here], owners))
        hidden = jnp.concatenate(pieces, 1)
        inner = hidden[:, depth : depth + height * depth]
        back_hidden[x] = (live_line(lanes, x, height) * inner).astype(bf16)
        send(x).start()
        conv = (hidden * slopes[x].astype(f32)).astype(bf16)
        for y in range(wide_height):
            back_conv[x, y] = conv[:, y * depth : (y + 1) * depth]
        lines = []
        for b in range(REACH):
            parts = [empty] * b + [conv[:, depth : depth + height * depth]]
            lines.append(jnp.concatenate(parts + [empty] * (REACH - 1 - b), 1))
        stacked = jnp.concatenate(lines, 0)
        total = None
        for y in range(0, wide_height, 2):
            near = stacked[:, y * depth : (y + 2) * depth]
            term = by_last(columns(taps, x, y + 1, 2), near)
            total = term if total is None else total + term
        grad[...] += total
        return 0

    lax.fori_loop(0, rows, one_row, 0)
    face_low[...] = back_conv[0]
    face_high[...] = back_conv[rows - 1]
    packed[...] = jnp.zeros_like(packed)
    turned = grad[...].T
    for place, part in packed_parts(turned.shape):
        tall = part[0].stop - part[0].start
        width = part[1].stop - part[1].start
        packed[place[0] : place[0] + tall, place[1] : place[1] + width] = turned[part]
    wait_rows(send, rows)


def packed_parts(shape):
    height, width = shape
    full = width // LANES * LANES
    rest = width - full
    parts = []
    for left in range(0, full, LANES):
        parts.append(((left // LANES * height, 0), (slice(0, height), slice(left, left + LANES))))
    if rest:
        folds = LANES // rest
        step = height // folds
        for k in range(folds):
            source = (slice(k * step, (k + 1) * step), slice(full, width))
            parts.append(((full // LANES * height, k * rest), source))
    return parts


def unpack(packed, shape):
    height, width = shape
    full = width // LANES * LANES
    rest = width - full
    blocks = [packed[left // LANES * height :][:height] for left in range(0, full, LANES)]
    if rest:
        folds = LANES // rest
        step = height // folds
        tail = packed[full // LANES * height :][:step]
        blocks.append(tail.reshape(step, folds, rest).swapaxes(0, 1).reshape(height, rest))
    return jnp.concatenate(blocks, 1)


def backward_kernel(
    back_conv, x_low, x_high, hidden_in, lanes, weight, grad_out,
    grad, taps, faces, back_hidden, sent, faces_here, hidden_here
):
    rows, wide_height, channels, depth = back_conv.shape
    height = wide_height - 2
    send = row_copy(grad, grad_out, sent)
    get_low = pltpu.make_async_copy(x_low, faces.at[0], faces_here.at[0])
    get_high = pltpu.make_async_copy(x_high, faces.at[1], faces_here.at[1])
    get_low.start()
    get_high.start()
    fetch = row_copy(hidden_in, back_hidden, hidden_here)

    def ask(x, _):
        fetch(x).start()
        return 0

    lax.fori_loop(0, rows, ask, 0)

    def fill(x, _):
        store_taps(taps, x + 1, 0, back_conv[x])
        return 0

    lax.fori_loop(0, rows, fill, 0)
    get_low.wait()
    get_high.wait()
    store_taps(taps, 0, 0, faces[0])
    store_taps(taps, rows + 1, 0, faces[1])

    def one_row(x, _):
        live = live_line(lanes, x, height)
        found = convolve_row((taps,), weight[...], x, height)
        fetch(x).wait()
        result = live * (back_hidden[x].astype(f32) + found)
        tiles = [result[:, y * depth : (y + 1) * depth][None] for y in range(height)]
        grad[x] = jnp.swapaxes(jnp.concatenate(tiles, 0), 0, 1)
        send(x).start()
        return 0

    lax.fori_loop(0, rows, one_row, 0)
    wait_rows(send, rows)


def cost(micros):
    return pl.CostEstimate(
        flops=micros * 10**9, bytes_accessed=micros * 3 * 10**6, transcendentals=0
    )


def call(kernel, shapes, *operands, scratch=(), micros=2, far_in=(), far_out=(), fixed_in=()):
    fixed = pl.BlockSpec(memory_space=pltpu.HBM)
    here, there = pl.BlockSpec(memory_space=pltpu.VMEM), pl.BlockSpec(memory_space=pl.ANY)
    return pl.pallas_call(
        kernel,
        in_specs=[
            fixed if i in fixed_in else there if i in far_in else here
            for i in range(len(operands))
        ],
        out_specs=[fixed if i in far_out else here for i in range(len(shapes))],
        out_shape=[jax.ShapeDtypeStruct(shape, kind) for shape, kind in shapes],
        scratch_shapes=list(scratch),
        cost_estimate=cost(micros),
        compiler_params=pltpu.CompilerParams(vmem_limit_bytes=LIMIT),
    )(*operands)


def pass_on(low, high, axis):
    count = lax.axis_size(axis)
    up = [(i, i + 1) for i in range(count - 1)]
    down = [(i + 1, i) for i in range(count - 1)]
    return lax.ppermute(high, axis, up), lax.ppermute(low, axis, down)


def exchange(parts, axes):
    return lax.all_to_all(parts, axes, 0, 0, tiled=True)


def body(
    features,
    occupied,
    voxel_fragment,
    conv_weight,
    embed_weight,
    message_weight,
    update_weight,
    edge_source,
    edge_target,
    out_cotangent,
):
    rows, channels, height, depth = features.shape
    frag_dev, hid = out_cotangent.shape
    owners = lax.axis_size("beam")
    edge_count = edge_source.shape[0]
    plane = height * depth
    lanes = jnp.repeat(occupied, BLOCK, 2).astype(f32)
    gate = jnp.repeat(jnp.repeat(lanes, BLOCK, 0), BLOCK, 1).astype(bf16)

    split = conv_weight.reshape(channels, REACH, REACH, REACH, channels)
    stacked_shape = (REACH * channels, REACH * REACH * channels)
    stacked = split.transpose(2, 0, 1, 3, 4).reshape(stacked_shape)
    flipped = split[:, ::-1, ::-1, ::-1].transpose(2, 4, 1, 3, 0).reshape(stacked_shape)

    x_low, x_high = pass_on(
        features[0] * gate[0][None], features[-1] * gate[-1][None], "drift"
    )
    owner, local = owner_and_local(voxel_fragment, frag_dev)
    ends = []
    for edge, first in ((0, 0), (height - 1, height - RIM)):
        layers = slice(first, first + RIM)
        side = (features[:, :, layers] * gate[:, None, layers]).transpose(0, 2, 1, 3)
        outer = [x[:, layers].transpose(1, 0, 2) for x in (x_low, x_high)]
        notes = [owner[:, edge].astype(bf16), local[:, edge].astype(bf16), gate[:, edge]]
        notes.append(jnp.zeros((channels - 3 * rows, depth), bf16))
        flat = side.reshape(RIM * rows, channels, depth)
        ends.append(
            jnp.concatenate([outer[0], flat, outer[1], jnp.concatenate(notes, 0)[None]], 0)
        )
    y_low, y_high = pass_on(ends[0], ends[1], "beam")

    heads = -(-owners // 16) * 16
    line_shape = (rows, channels, plane)
    wide_shape = (rows, channels, plane + 2 * depth)
    conv_shape = (rows, height + 2, channels, depth)
    dma = lambda count: pltpu.SemaphoreType.DMA((count,))
    tapped = (rows + 2, height + 2, REACH * channels, depth)
    inner_shape = (rows + 2, height, REACH * channels, depth)
    rim_shape = (rows + 2, RIM, REACH * channels, depth)
    (core,) = call(
        inner_kernel, [(inner_shape, bf16)], features, x_low, x_high, lanes, micros=3
    )
    low, high, slopes, partial, sides = call(
        forward_kernel,
        [
            (rim_shape, bf16),
            (rim_shape, bf16),
            (wide_shape, bf16),
            ((owners, channels + SPARE, frag_dev), bf16),
            ((2, channels, depth), f32),
        ],
        core, y_low, y_high, lanes, voxel_fragment, stacked, micros=9,
        scratch=[
            pltpu.VMEM((owners * channels + heads, frag_dev), f32),
            pltpu.VMEM((2,) + y_low.shape, bf16), dma(2),
        ],
        far_in=(1, 2),
    )
    spread_shape = (owners, channels, frag_dev)
    pooled, divisor = call(
        pool_kernel,
        [(spread_shape, bf16), ((8, frag_dev), f32)],
        exchange(partial, "beam"),
    )
    table = exchange(pooled, "beam")
    fragment_out, back_parts, direct = call(
        fragment_kernel,
        [((frag_dev, hid), bf16), (spread_shape, bf16), ((channels, frag_dev), f32)],
        table, pooled[0], embed_weight, message_weight, update_weight, out_cotangent,
        edge_source.reshape(1, edge_count),
        edge_target.reshape(1, edge_count), flipped, far_in=(8,),
    )
    (mean,) = call(
        mean_kernel, [(spread_shape, bf16)], exchange(back_parts, "beam"), direct, divisor
    )
    everyone = ("drift", "beam")
    devices = lax.axis_size(everyone)
    tile = SUBLANES * LANES
    share = -(-conv_weight.size // (devices * tile)) * SUBLANES
    back_hidden, back_conv, face_low, face_high, packed = call(
        hidden_kernel,
        [
            (line_shape, bf16), (conv_shape, bf16), (conv_shape[1:], bf16), (conv_shape[1:], bf16),
            ((devices * share, LANES), f32),
        ],
        exchange(mean, "beam"), voxel_fragment, lanes, sides, slopes, low, core, high, micros=9,
        scratch=[
            pltpu.VMEM(stacked_shape[::-1], f32), pltpu.VMEM(line_shape, bf16), dma(rows),
        ],
        far_out=(0,),
    )
    gx_low, gx_high = pass_on(face_low, face_high, "drift")
    (grad_features,) = call(
        backward_kernel,
        [(features.shape, f32)],
        back_conv, gx_low, gx_high, back_hidden, lanes, flipped, micros=10,
        scratch=[
            pltpu.VMEM(features.shape, f32), pltpu.VMEM(tapped, bf16),
            pltpu.VMEM((2,) + conv_shape[1:], bf16), pltpu.VMEM(line_shape, bf16),
            dma(rows), dma(2), dma(rows),
        ],
        far_in=(1, 2), fixed_in=(3,), far_out=(0,),
    )
    parts = exchange(packed, everyone).reshape(devices, share, LANES)
    full = exchange(jnp.broadcast_to(parts.sum(0)[None], parts.shape), everyone)
    grad_conv = (
        unpack(full.reshape(devices * share, LANES), stacked_shape)
        .reshape(REACH, channels, REACH, REACH, channels)
        .transpose(1, 2, 0, 3, 4)
        .reshape(conv_weight.shape)
    )
    return fragment_out, grad_features, grad_conv


def solution(mesh):
    return jax.shard_map(
        body,
        mesh=mesh,
        in_specs=(
            P("drift", None, "beam", None),
            P("drift", "beam", None),
            P("drift", "beam", None),
            P(),
            P(),
            P(),
            P(),
            P(("drift", "beam")),
            P(("drift", "beam")),
            P(("drift", "beam"), None),
        ),
        out_specs=(P(("drift", "beam"), None), P("drift", None, "beam", None), P()),
        check_vma=False,
    )
```
